32 devices in a mesh: dp: 32 (over z, y, x, core).
Axes of the slice: x: 2, y: 2, z: 4, core: 2. Of those that a mesh axis runs over, the one named last changes fastest.
Arguments:
- block_in: bfloat16 [65536, 256], P('dp'), may hold values from -6 to 6
- lengths: int32 [64], P('dp'), may hold values from 204 to 1024, as said below
- back_w: bfloat16 [512, 256], P('dp'), may hold values from -0.25 to 0.25
- back_b: bfloat16 [256], P('dp'), may hold values from -3 to 3
- heads_w: bfloat16 [256, 768], P('dp'), may hold values from -0.375 to 0.375
- heads_b: bfloat16 [768], P('dp'), may hold values from -5 to 2
- norm1_gain: bfloat16 [256], P('dp'), may hold values from 0.099609375 to 1.8984375
- norm1_bias: bfloat16 [256], P('dp'), may hold values from -2.5 to 2.5
- norm2_gain: bfloat16 [256], P('dp'), may hold values from 0.099609375 to 1.8984375
- norm2_bias: bfloat16 [256], P('dp'), may hold values from -2.5 to 2.5
- up_w: bfloat16 [256, 1024], P('dp'), may hold values from -0.375 to 0.375
- up_b: bfloat16 [1024], P('dp'), may hold values from -3 to 3
- down_w: bfloat16 [1024, 256], P('dp'), may hold values from -0.375 to 0.375
- down_b: bfloat16 [256], P('dp'), may hold values from -2.5 to 2.5
- cotangent: bfloat16 [65536, 256], P('dp'), may hold values from -6 to 6
Outputs:
- block_out: bfloat16 [65536, 256], P('dp')
- input_grad: bfloat16 [65536, 256], P('dp')
- backward_weight_gradient: float32 [512, 256], P('dp')
- grad_back_b: float32 [256], P('dp')
- grad_heads_w: float32 [256, 768], P('dp')
- grad_heads_b: float32 [768], P('dp')
- grad_norm1_gain: float32 [256], P('dp')
- grad_norm1_bias: float32 [256], P('dp')
- grad_norm2_gain: float32 [256], P('dp')
- grad_norm2_bias: float32 [256], P('dp')
- grad_up_w: float32 [256, 1024], P('dp')
- grad_up_b: float32 [1024], P('dp')
- grad_down_w: float32 [1024, 256], P('dp')
- grad_down_b: float32 [256], P('dp')
The draws below stay inside these ranges and needn't reach their ends.
Inputs may be any that keep to these rules, and one draw needn't show every extreme that they name: `lengths`: one sequence has exactly 1024 live steps in every draw.
All inputs are finite; a program needn't handle non-finite values.
Results may differ from the reference program's by a relative error of at most 0.0063.
Values may be sent and summed in bfloat16 or wider, within the bound.
A program may use at most 128 MiB of HBM per device.

```python
import math
import jax
import jax.numpy as jnp
from jax import lax

D = 256
FF = 1024
SPAN = 64
LENGTH = 1024
SEQS = 64
TOKEN_TOTAL = 65536


def draw_lengths(key, part):
    key = jax.random.fold_in(key, 5)
    key_values, key_chosen = jax.random.split(key)
    values = jax.random.randint(key_values, (SEQS,), LENGTH // 5, LENGTH + 1)
    chosen = jax.random.randint(key_chosen, (), 0, SEQS)
    return jnp.where(jnp.arange(SEQS) == chosen, LENGTH, values).astype(jnp.int32)


def draw_heads_b(key, part):
    key = jax.random.fold_in(key, 11)
    key_rates, key_rest = jax.random.split(key)
    rate_bias = jax.random.uniform(key_rates, (D,), jnp.float32, -4.0, 1.0)
    value_bias = jnp.clip(0.5 * jax.random.normal(key_rest, (2 * D,), jnp.float32), -2.0, 2.0)
    return jnp.concatenate([rate_bias, value_bias]).astype(jnp.bfloat16)


def levels(own_key, extent, cuts, low, largest):
    gain, own = 1.0, jax.random.fold_in(own_key, 6)
    for dim, blocks in cuts:
        steps = jnp.exp(jax.random.uniform(jax.random.fold_in(own, dim), (blocks,), jnp.float32, low / len(cuts), largest / len(cuts)))
        gain = gain * jnp.repeat(steps, extent[dim] // blocks).reshape([-1 if axis == dim else 1 for axis in range(len(extent))])
    return gain


def gaussian(rng, dims, spread, most, cuts=(), kind=jnp.bfloat16):
    result = spread * jax.random.normal(rng, dims, jnp.float32)
    if cuts:
        result = result * levels(rng, dims, cuts, -0.22, 0.18)
    return jnp.clip(result, -most, most).astype(kind)


def setup_inputs(seed: int = 0) -> dict:
    streams_of = jax.random.split(jax.random.key(seed), 16)
    block_in = gaussian(streams_of[0], (TOKEN_TOTAL, D), 1.0, 6.0, ((0, 32),))
    lengths = draw_lengths(jax.random.fold_in(streams_of[15], 71), 0)
    back_w = gaussian(streams_of[2], (2 * D, D), (2 * D) ** -0.5, 0.25, ((0, 32),))
    back_b = gaussian(streams_of[3], (D,), 0.5, 3.0, ((0, 32),))
    heads_w = gaussian(streams_of[4], (D, 3 * D), D ** -0.5, 0.375, ((0, 32),))
    heads_b = draw_heads_b(jax.random.fold_in(streams_of[15], 71), 0)
    norm1_gain = jnp.clip(1.0 + 0.18 * jax.random.normal(streams_of[6], (D,), jnp.float32), 0.099609375, 1.8984375).astype(jnp.bfloat16)
    norm1_bias = gaussian(streams_of[7], (D,), 0.4, 2.5, ((0, 32),))
    norm2_gain = jnp.clip(1.0 + 0.18 * jax.random.normal(streams_of[8], (D,), jnp.float32), 0.099609375, 1.8984375).astype(jnp.bfloat16)
    norm2_bias = gaussian(streams_of[9], (D,), 0.4, 2.5, ((0, 32),))
    up_w = gaussian(streams_of[10], (D, FF), D ** -0.5, 0.375, ((0, 32),))
    up_b = gaussian(streams_of[11], (FF,), 0.5, 3.0, ((0, 32),))
    down_w = gaussian(streams_of[12], (FF, D), (FF // 4) ** -0.5, 0.375, ((0, 32),))
    down_b = gaussian(streams_of[13], (D,), 0.4, 2.5, ((0, 32),))
    cotangent = gaussian(streams_of[14], (TOKEN_TOTAL, D), 1.0, 6.0, ((0, 32),))
    return {"block_in": block_in, "lengths": lengths, "back_w": back_w, "back_b": back_b, "heads_w": heads_w, "heads_b": heads_b, "norm1_gain": norm1_gain, "norm1_bias": norm1_bias, "norm2_gain": norm2_gain, "norm2_bias": norm2_bias, "up_w": up_w, "up_b": up_b, "down_w": down_w, "down_b": down_b, "cotangent": cotangent}


@jax.custom_vjp
def low(v):
    return lax.optimization_barrier(v.astype(jnp.bfloat16)).astype(jnp.float32)

@jax.custom_vjp
def low_back(v):
    return v

def low_keep(v):
    return (low(v), None)

def low_pass(kept, grad):
    return (grad,)

def back_keep(v):
    return (v, None)

def back_low(kept, grad):
    return (low(grad),)
low.defvjp(low_keep, low_pass)
low_back.defvjp(back_keep, back_low)

def lecun_tanh(values):
    return 1.7159 * jnp.tanh(0.666 * values)

def layer_norm(values, norm_gain, norm_shift):
    row_mean = lax.optimization_barrier(jnp.mean(values, axis=-1, keepdims=True))
    centered = values - row_mean
    variance = lax.optimization_barrier(jnp.mean(centered * centered, axis=-1, keepdims=True))
    return centered * lax.rsqrt(variance + 1e-05) * norm_gain + norm_shift

def matmul(left, right):
    return jnp.matmul(left, right, precision=lax.Precision.HIGHEST)

def block_scan(running_state, pieces):
    log_keep, forcing_term = pieces
    block_len = log_keep.shape[1]
    summed_logarithm = jnp.cumsum(log_keep, axis=1)
    log_ratio = summed_logarithm[:, :, None, :] - summed_logarithm[:, None, :, :]
    causal = (jnp.arange(block_len)[:, None] >= jnp.arange(block_len)[None, :])[None, :, :, None]
    weight_tree = jnp.where(causal, jnp.exp(jnp.where(causal, log_ratio, 0.0)), 0.0)
    final_output = jnp.einsum('enfp,efp->enp', weight_tree, forcing_term) + jnp.exp(summed_logarithm) * running_state[:, None, :]
    return (final_output[:, -1, :], final_output)

def run_blocks(log_keep, forcing_term):
    seq_count, length, model_width = log_keep.shape
    block_count = length // SPAN
    shaped = (seq_count, block_count, SPAN, model_width)
    keep_blocks = log_keep.reshape(shaped).transpose(1, 0, 2, 3)
    drive_blocks = forcing_term.reshape(shaped).transpose(1, 0, 2, 3)
    start = jnp.zeros((seq_count, model_width), log_keep.dtype)
    final_state, states = lax.scan(jax.checkpoint(block_scan), start, (keep_blocks, drive_blocks))
    return states.transpose(1, 0, 2, 3).reshape(seq_count, length, model_width)

def cell_tail(pre_heads, norm_gain, norm_shift, validity):
    model_width = norm_gain.shape[0]
    rate = pre_heads[..., :model_width]
    value_head = jnp.tanh(pre_heads[..., model_width:2 * model_width])
    fallback = jnp.tanh(pre_heads[..., 2 * model_width:])
    opened = jax.nn.sigmoid(rate)
    log_keep = jnp.log1p(-validity * opened)
    forcing_term = validity * (opened * value_head + (1.0 - opened) * fallback)
    states = run_blocks(log_keep, forcing_term)
    return validity * layer_norm(states, norm_gain, norm_shift)

def group_forward(inputs, lengths, params):
    back_w, back_b, heads_w, heads_b, gain_one, bias_one, gain_two, bias_two, up_w, up_b, down_w, down_b = params
    positions = jnp.arange(LENGTH, dtype=jnp.int32)
    validity = (positions[None, :] < lengths[:, None]).astype(jnp.float32)[:, :, None]
    previous = jnp.concatenate([jnp.zeros_like(inputs[:, :1]), inputs[:, :-1]], axis=1)
    joined = jnp.concatenate([inputs, previous], axis=-1)
    pre_back = low_back(matmul(joined, back_w) + back_b)
    features = low(lecun_tanh(pre_back))
    pre_heads = low_back(matmul(features, heads_w) + heads_b)
    mid = inputs + cell_tail(pre_heads, gain_one, bias_one, validity)
    normed = low(layer_norm(mid, gain_two, bias_two))
    pre_up = low_back(matmul(normed, up_w) + up_b)
    hidden = low(jax.nn.gelu(pre_up, approximate=True))
    return mid + validity * (matmul(hidden, down_w) + down_b)

def forward(inputs, lengths, params):
    group_size = math.gcd(SEQS, max(1, 4096 // LENGTH))
    stacked = inputs.reshape(SEQS // group_size, group_size, LENGTH, D)
    grouped = lengths.reshape(SEQS // group_size, group_size)

    def one_group(member):
        return group_forward(member[0], member[1], params)
    final_output = lax.map(jax.checkpoint(one_group), (stacked, grouped))
    return final_output.reshape(SEQS * LENGTH, D)

def reference(block_in, lengths, back_w, back_b, heads_w, heads_b, norm1_gain, norm1_bias, norm2_gain, norm2_bias, up_w, up_b, down_w, down_b, cotangent):
    params = tuple((item.astype(jnp.float32) for item in (back_w, back_b, heads_w, heads_b, norm1_gain, norm1_bias, norm2_gain, norm2_bias, up_w, up_b, down_w, down_b)))
    inputs = block_in.astype(jnp.float32)

    def whole(input_values, param_values):
        return forward(input_values, lengths, param_values)
    final_output, pull = jax.vjp(whole, inputs, params)
    grad_in, grads = pull(cotangent.astype(jnp.float32))
    return (final_output.astype(jnp.bfloat16), grad_in.astype(jnp.bfloat16), grads[0], grads[1], grads[2], grads[3], grads[4], grads[5], grads[6], grads[7], grads[8], grads[9], grads[10], grads[11])
```

```python
import functools
import jax
import jax.numpy as jnp
from jax import lax
from jax.experimental import pallas as pl
from jax.experimental.pallas import tpu as pltpu
from jax.sharding import PartitionSpec as P

BLK = 256
LANES = 8
STEPS = BLK // LANES
QUAD = 4
FF_STEP = 256
F32 = jnp.float32
BF16 = jnp.bfloat16
MESH = pl.DeviceIdType.MESH
GC = 0.7978845608028654
GA = 0.044715


def mm(a, b):
    return lax.dot_general(a, b, (((1,), (0,)), ((), ())), preferred_element_type=F32)


def mm_nt(a, b):
    return lax.dot_general(a, b, (((1,), (1,)), ((), ())), preferred_element_type=F32)


def mm_tn(a, b):
    return lax.dot_general(a, b, (((0,), (0,)), ((), ())), preferred_element_type=F32)


def shuffle(transposed=False):
    row = lax.broadcasted_iota(jnp.int32, (BLK, BLK), 0)
    col = lax.broadcasted_iota(jnp.int32, (BLK, BLK), 1)
    if transposed:
        row, col = col, row
    return jnp.where((row & 7) * STEPS + (row >> 3) == col, 1.0, 0.0).astype(BF16)


def fold(values):
    return jnp.sum(values.reshape(values.shape[0] // 8, 8, values.shape[1]), axis=0)


def sublane(shape):
    return lax.broadcasted_iota(jnp.int32, shape, 0)


def flat(ref):
    values = ref[...]
    return values.reshape(-1, values.shape[-1])


def block_rows(i, dims):
    return pl.ds(i * (dims[0] * BLK), dims[0] * BLK)


def enter(i, r, dims):
    S, L, D = dims
    order = shuffle()
    sub = sublane((8, D))
    joined = []
    for s in range(S):
        mixed = mm(order, r.x[pl.ds(s * L + i * BLK, BLK), :])
        turned = pltpu.roll(mixed[BLK - 8 :], 1, 0)
        first = jnp.where(sub == 0, jnp.where(i == 0, 0.0, r.xcarry[s]), turned)
        r.xcarry[s] = turned
        before = jnp.concatenate([first, mixed[: BLK - 8]], axis=0)
        joined.append(jnp.concatenate([mixed, before], axis=1))
    r.joined[block_rows(i, dims), :] = jnp.concatenate(joined, axis=0).astype(BF16)


def backbone(i, r, dims):
    rows = block_rows(i, dims)
    inner = jnp.tanh(0.666 * (mm(r.joined[rows, :], flat(r.wb)) + r.bb[...]))
    r.inner[rows, :] = inner
    r.feat[rows, :] = (1.7159 * inner).astype(BF16)


def gates(i, r, dims):
    S, L, D = dims
    rows = block_rows(i, dims)
    sub = sublane((8, D))
    heads = mm(r.feat[rows, :], r.wh[...]) + r.bh[...]
    o = 0.5 * jnp.tanh(0.5 * heads[:, :D]) + 0.5
    v = jnp.tanh(heads[:, D : 2 * D])
    f = jnp.tanh(heads[:, 2 * D :])
    r.o[rows, :] = o
    r.v[rows, :] = v
    r.f[rows, :] = f
    keep = 1.0 - o
    drive = f + o * (v - f)
    one = jnp.ones((8, D), F32)
    for s in range(S):
        k = [keep[s * BLK + 8 * j : s * BLK + 8 * j + 8] for j in range(STEPS)]
        d = [drive[s * BLK + 8 * j : s * BLK + 8 * j + 8] for j in range(STEPS)]
        A, Q = k[0], d[0]
        for j in range(1, STEPS):
            Q = k[j] * Q + d[j]
            A = k[j] * A
        for sh in (1, 2, 4):
            An = jnp.where(sub < sh, one, pltpu.roll(A, sh, 0))
            Qn = jnp.where(sub < sh, 0.0, pltpu.roll(Q, sh, 0))
            Q = Q + A * Qn
            A = A * An
        carry = jnp.where(i == 0, 0.0, r.scarry[s])
        ends = Q + A * carry
        start = jnp.where(sub == 0, carry, pltpu.roll(ends, 1, 0))
        r.scarry[s] = jnp.broadcast_to(ends[7:8], (8, D))
        r.start[i, s] = start
        Q = start
        for j in range(STEPS):
            Q = k[j] * Q + d[j]
            r.state[pl.ds(i * (S * BLK) + s * BLK + 8 * j, 8), :] = Q


def live(i, r, dims):
    S, L, D = dims
    row = lax.broadcasted_iota(jnp.int32, (BLK, D), 0)
    time = (row & 7) * STEPS + (row >> 3) + i * BLK
    return jnp.concatenate([time < r.lengths[s] for s in range(S)], axis=0)


def normalise(values, D):
    mean = jnp.sum(values, axis=1, keepdims=True) * (1.0 / D)
    c = values - mean
    var = jnp.sum(c * c, axis=1, keepdims=True) * (1.0 / D)
    rs = lax.rsqrt(var + 1e-05)
    return c * rs, rs


def norm_back(dy, gain, xhat, rs, D):
    dx = dy * gain
    m1 = jnp.sum(dx, axis=1, keepdims=True) * (1.0 / D)
    m2 = jnp.sum(dx * xhat, axis=1, keepdims=True) * (1.0 / D)
    return rs * (dx - m1 - xhat * m2)


def feed_forward(i, r, dims):
    S, L, D = dims
    FF = r.wu.shape[1]
    rows = block_rows(i, dims)
    order, back = shuffle(), shuffle(True)
    valid = live(i, r, dims)
    g1, b1, g2, b2 = r.g1[...], r.b1[...], r.g2[...], r.b2[...]
    xhat1, rs1 = normalise(r.state[rows, :], D)
    mid = r.joined[rows, pl.ds(0, D)].astype(F32) + jnp.where(valid, xhat1 * g1 + b1, 0.0)
    xhat2, rs2 = normalise(mid, D)
    normed = (xhat2 * g2 + b2).astype(BF16)
    r.normed[rows, :] = normed
    cot = jnp.concatenate([mm(order, r.cot[pl.ds(s * L + i * BLK, BLK), :]) for s in range(S)], axis=0)
    gout32 = jnp.where(valid, cot, 0.0)
    r.gbd[...] += fold(gout32)
    gout = gout32.astype(BF16)
    r.gout[rows, :] = gout
    W = FF_STEP
    y = gn = None
    for n in range(FF // W):
        cols = slice(n * W, (n + 1) * W)
        down = r.wd_rows(n, W)
        pu = mm(normed, r.wu[:, cols]) + r.bu[:, cols]
        v2 = pu * pu
        h = 0.5 * jnp.tanh(pu * (v2 * (GC * GA) + GC)) + 0.5
        hid = pu * h
        hid16 = hid.astype(BF16)
        r.hidden[rows, cols] = hid16
        slope = h + hid * (1.0 - h) * (v2 * (6.0 * GA * GC) + 2.0 * GC)
        gpu = (mm_nt(gout, down) * slope).astype(BF16)
        r.gpu[rows, cols] = gpu
        r.gbu[:, cols] += fold(gpu.astype(F32))
        yn = mm(hid16, down)
        gnn = mm_nt(gpu, r.wu[:, cols])
        y = yn if y is None else y + yn
        gn = gnn if gn is None else gn + gnn
    out = (mid + jnp.where(valid, y + r.bd[...], 0.0)).astype(BF16)
    for s in range(S):
        r.out[pl.ds(s * L + i * BLK, BLK), :] = mm(back, out[s * BLK : (s + 1) * BLK]).astype(BF16)
    r.gg2[...] += fold(gn * xhat2)
    r.gb2[...] += fold(gn)
    gmid = cot + norm_back(gn, g2, xhat2, rs2, D)
    r.gmid[rows, :] = gmid
    dy1 = jnp.where(valid, gmid, 0.0)
    r.gg1[...] += fold(dy1 * xhat1)
    r.gb1[...] += fold(dy1)
    r.gnorm[rows, :] = norm_back(dy1, g1, xhat1, rs1, D)


def gates_back(i, r, dims):
    S, L, D = dims
    nb = L // BLK
    rows = block_rows(i, dims)
    sub = sublane((8, D))
    o = r.o[rows, :]
    keep = 1.0 - o
    gnorm = r.gnorm[rows, :]
    state = r.state[rows, :]
    gss, sps = [], []
    one = jnp.ones((8, D), F32)
    for s in range(S):
        k = [keep[s * BLK + 8 * j : s * BLK + 8 * j + 8] for j in range(STEPS)]
        g = [gnorm[s * BLK + 8 * j : s * BLK + 8 * j + 8] for j in range(STEPS)]
        A = k[STEPS - 1]
        H = k[STEPS - 1] * g[STEPS - 1]
        for j in range(STEPS - 2, -1, -1):
            H = k[j] * (g[j] + H)
            A = k[j] * A
        for sh in (1, 2, 4):
            An = jnp.where(sub >= 8 - sh, one, pltpu.roll(A, 8 - sh, 0))
            Hn = jnp.where(sub >= 8 - sh, 0.0, pltpu.roll(H, 8 - sh, 0))
            H = H + A * Hn
            A = A * An
        carry = jnp.where(i == nb - 1, 0.0, r.scarry[s])
        ends = H + A * carry
        r.scarry[s] = jnp.broadcast_to(ends[0:1], (8, D))
        H = jnp.where(sub == 7, carry, pltpu.roll(ends, 7, 0))
        out = [None] * STEPS
        for j in range(STEPS - 1, -1, -1):
            G = g[j] + H
            H = k[j] * G
            out[j] = G
        gss += out
        sps += [r.start[i, s], state[s * BLK : (s + 1) * BLK - 8]]
    gs = jnp.concatenate(gss, axis=0)
    sp = jnp.concatenate(sps, axis=0)
    v = r.v[rows, :]
    f = r.f[rows, :]
    go = gs * o
    grate = go * keep * (v - f - sp)
    gv = go * (1.0 - v * v)
    gf = (gs - go) * (1.0 - f * f)
    gph = jnp.concatenate([grate, gv, gf], axis=1).astype(BF16)
    r.gph[rows, :] = gph
    r.gbh[...] += fold(gph.astype(F32))
    inner = r.inner[rows, :]
    gpb = (mm_nt(gph, r.wh[...]) * ((1.7159 * 0.666) * (1.0 - inner * inner))).astype(BF16)
    r.gpb[rows, :] = gpb
    r.gbb[...] += fold(gpb.astype(F32))


def leave(i, r, dims):
    S, L, D = dims
    nb = L // BLK
    rows = block_rows(i, dims)
    sub = sublane((8, D))
    back = shuffle(True)
    gj = mm_nt(r.gpb[rows, :], flat(r.wb))
    gmid = r.gmid[rows, :]
    for s in range(S):
        own = gj[s * BLK : (s + 1) * BLK, :D]
        before = gj[s * BLK : (s + 1) * BLK, D:]
        turned = pltpu.roll(before[:8], 7, 0)
        last = jnp.where(sub == 7, jnp.where(i == nb - 1, 0.0, r.xcarry[s]), turned)
        r.xcarry[s] = turned
        moved = jnp.concatenate([before[8:], last], axis=0)
        grad = (gmid[s * BLK : (s + 1) * BLK] + own + moved).astype(BF16)
        r.ig[pl.ds(s * L + i * BLK, BLK), :] = mm(back, grad).astype(BF16)


SUMS = ("gbb", "gbh", "gg1", "gb1", "gg2", "gb2", "gbu", "gbd")


def zero_sums(r):
    for name in SUMS:
        ref = getattr(r, name)
        ref[...] = jnp.zeros_like(ref)


def sum_widths(D, FF):
    return (D, 3 * D, D, D, D, D, FF, D)


def work_space(S, L, D, FF):
    T = S * L
    v = pltpu.VMEM
    space = dict(
        joined=v((T, 2 * D), BF16), inner=v((T, D), F32), feat=v((T, D), BF16),
        o=v((T, D), F32), v=v((T, D), F32), f=v((T, D), F32), state=v((T, D), F32),
        start=v((L // BLK, S, 8, D), F32), xcarry=v((S, 8, D), F32), scarry=v((S, 8, D), F32),
        normed=v((T, D), BF16), gout=v((T, D), BF16), hidden=v((T, FF), BF16), gpu=v((T, FF), BF16),
        gmid=v((T, D), F32), gnorm=v((T, D), F32), gph=v((T, 3 * D), BF16), gpb=v((T, D), BF16),
    )
    for name, width in zip(SUMS, sum_widths(D, FF)):
        space[name] = v((8, width), F32)
    return space


class Refs:
    def wd_rows(self, n, width):
        if len(self.wd.shape) == 2:
            return self.wd[pl.ds(n * width, width), :]
        z, q, c, piece, columns = self.wd.shape
        plane = q * c * piece
        return self.wd[pl.ds(n * width // plane, width // plane)].reshape(width, columns)


def refs_of(names, refs):
    r = Refs()
    for name, ref in zip(names, refs):
        setattr(r, name, ref)
    return r


class Place:
    def __init__(self, n):
        self.n = n
        self.planes = n // (2 * QUAD)
        self.me = lax.axis_index("dp")
        self.c = self.me % 2
        self.q = (self.me // 2) % QUAD
        self.z = self.me // (2 * QUAD)
        self.partner = self.me + 1 - 2 * self.c

    def plane(self, k):
        return (self.z + k) % self.planes

    def corner(self, k):
        return (self.q + k) % QUAD

    def device(self, z, q):
        return (z * QUAD + q) * 2 + self.c

    def others(self):
        return [(a, b) for a in range(self.planes) for b in range(QUAD) if a or b]


class Copies:
    def __init__(self, send, recv):
        self.send, self.recv, self.used, self.open = send, recv, 0, []

    def start(self, src, dst, device):
        k = self.used
        self.used += 1
        copy = pltpu.make_async_remote_copy(
            src_ref=src, dst_ref=dst, send_sem=self.send.at[k], recv_sem=self.recv.at[k],
            device_id=(device,), device_id_type=MESH,
        )
        copy.start()
        self.open.append(copy)
        return copy

    def finish(self):
        for copy in self.open:
            copy.wait_send()


def arrived(copies):
    for copy in copies:
        copy.wait_recv()


def cut(values):
    half = values.shape[-1] // 2
    return jnp.concatenate([values[..., :half], values[..., half:]], axis=-2)


def uncut(values):
    return jnp.concatenate([values[..., :8, :], values[..., 8:, :]], axis=-1)


def same(values):
    return values


class Share:
    def __init__(self, r, name, cutter, copies, place, direct):
        self.r, self.name, self.cut, self.copies, self.p, self.direct = r, name, cutter, copies, place, direct

    def ref(self, kind):
        return getattr(self.r, kind + self.name)

    def pair(self):
        p = self.p
        self.ref("cs")[...] = self.cut(self.ref("dw")[:, :, 1 - p.c]).astype(BF16)
        self.paired = self.copies.start(self.ref("cs"), self.ref("cr"), p.partner)

    def spread(self):
        p = self.p
        self.paired.wait_recv()
        total = self.cut(self.ref("dw")[:, :, p.c]) + self.ref("cr")[...].astype(F32)
        xs = self.ref("xs")
        xs[...] = total.astype(BF16)
        self.sent = []
        if self.direct:
            for k, (a, b) in enumerate(p.others()):
                z, q = p.plane(a), p.corner(b)
                self.sent.append(self.copies.start(xs.at[z, q], self.ref("xr").at[k], p.device(z, q)))
        else:
            for b in range(1, QUAD):
                q = p.corner(b)
                self.sent.append(self.copies.start(xs.at[:, q], self.ref("xr").at[b - 1], p.device(p.z, q)))

    def climb(self):
        p = self.p
        arrived(self.sent)
        acc = self.cut(self.ref("dw")[:, p.q, p.c]) + self.ref("cr")[:, p.q].astype(F32)
        for b in range(QUAD - 1):
            acc = acc + self.ref("xr")[b].astype(F32)
        self.ref("ac")[...] = acc
        self.ref("zs")[...] = acc.astype(BF16)
        self.sent = []
        for a in range(1, p.planes):
            z = p.plane(a)
            self.sent.append(self.copies.start(self.ref("zs").at[z], self.ref("zr").at[a - 1], p.device(z, p.q)))

    def land(self):
        p = self.p
        arrived(self.sent)
        if self.direct:
            acc = self.cut(self.ref("dw")[p.z, p.q, p.c]) + self.ref("cr")[p.z, p.q].astype(F32)
            for k in range(len(self.sent)):
                acc = acc + self.ref("xr")[k].astype(F32)
        else:
            acc = self.ref("ac")[p.z]
            for k in range(len(self.sent)):
                acc = acc + self.ref("zr")[k].astype(F32)
        return acc


def share_space(name, n, rows, columns, cutting, direct):
    Z, v = n // (2 * QUAD), pltpu.VMEM
    R, C = (2 * rows, columns // 2) if cutting else (rows, columns)
    space = {
        "dw" + name: v((Z, QUAD, 2, rows, columns), F32),
        "cs" + name: v((Z, QUAD, R, C), BF16),
        "cr" + name: v((Z, QUAD, R, C), BF16),
        "xs" + name: v((Z, QUAD, R, C), BF16),
    }
    if direct:
        space["xr" + name] = v((Z * QUAD - 1, R, C), BF16)
    else:
        space["xr" + name] = v((QUAD - 1, Z, R, C), BF16)
        space["ac" + name] = v((Z, R, C), F32)
        space["zs" + name] = v((Z, R, C), BF16)
        space["zr" + name] = v((Z - 1, R, C), BF16)
    return space


def segments(n, D, FF):
    found, lane, offset = [], 0, 0
    for name, width in zip(("bb", "bh", "g1", "b1", "g2", "b2", "bu", "bd"), sum_widths(D, FF)):
        found.append((name, lane, width, width // n, offset))
        lane, offset = lane + width, offset + width // n
    return found


def fill_pick(r, n, D, FF):
    for name, lane, width, own, offset in segments(n, D, FF):
        l = lax.broadcasted_iota(jnp.int32, (width, 128), 0).astype(F32)
        k = lax.broadcasted_iota(jnp.int32, (width, 128), 1).astype(F32)
        place = l - own * jnp.floor((l + 0.5) * (1.0 / own)) + offset
        r.pick[pl.ds(lane, width), :] = jnp.where(place == k, 1.0, 0.0).astype(BF16)


def owners(n, D, FF):
    parts = []
    for name, lane, width, own, offset in segments(n, D, FF):
        l = lax.broadcasted_iota(jnp.int32, (n, width), 1).astype(F32)
        row = lax.broadcasted_iota(jnp.int32, (n, width), 0)
        device = (2 * (row % (n // 2)) + row // (n // 2)).astype(F32)
        parts.append(jnp.floor((l + 0.5) * (1.0 / own)) == device)
    return jnp.concatenate(parts, axis=1)


ROWS = ("gback", "gheads", "gup", "gdown", "gvec")
INPUTS = ("lengths", "x_hbm", "cot_hbm", "wb_own", "wh_own", "wu_own", "wd_own", "vec_own")
OUTPUTS = ("out_hbm", "ig_hbm") + ROWS


def mega(names, dims, n, FF, *refs):
    r = refs_of(names, refs)
    S, L, D = dims
    nb = L // BLK
    p = Place(n)
    chips = n // 2
    chip = p.z * QUAD + p.q
    copies = Copies(r.send, r.recv)

    def run(f, first, last, down=False):
        def step(i, c):
            f(nb - 1 - i if down else i, r, dims)
            return c
        lax.fori_loop(first, last, step, 0)

    barrier = pltpu.get_barrier_semaphore()
    for a, b in p.others():
        pl.semaphore_signal(barrier, inc=1, device_id=(p.device(p.plane(a), p.corner(b)),), device_id_type=MESH)
    pl.semaphore_signal(barrier, inc=1, device_id=(p.partner,), device_id_type=MESH)

    loads = [
        pltpu.make_async_copy(src, dst, r.local.at[k])
        for k, (src, dst) in enumerate((
            (r.wb_own, r.wb.at[p.z, p.q, p.c]), (r.vec_own, r.vec.at[p.c, pl.ds(chip, 1)]),
            (r.wh_own, r.wh_mine), (r.wu_own, r.wu_mine), (r.wd_own, r.wd.at[p.z, p.q, p.c]),
            (r.x_hbm, r.x), (r.cot_hbm, r.cot),
        ))
    ]
    for load in loads:
        load.start()
    for load in loads[:5]:
        load.wait()
    r.wh_cut[p.z, p.q, p.c] = cut(r.wh_mine[...].astype(F32)).astype(BF16)
    r.wu_cut[p.z, p.q, p.c] = cut(r.wu_mine[...].astype(F32)).astype(BF16)
    pl.semaphore_wait(barrier, len(p.others()) + 1)

    def send_all(ref):
        return [
            copies.start(ref.at[p.z, p.q, p.c], ref.at[p.z, p.q, p.c], p.device(p.plane(a), p.corner(b)))
            for a, b in p.others()
        ]

    def send_planes(ref):
        return [
            copies.start(ref.at[p.z, p.q, p.c], ref.at[p.z, p.q, p.c], p.device(p.plane(a), p.q))
            for a in range(1, p.planes)
        ]

    def send_corners(ref):
        return [
            copies.start(ref.at[:, p.q, p.c], ref.at[:, p.q, p.c], p.device(p.z, p.corner(b)))
            for b in range(1, QUAD)
        ]

    def send_pair(ref):
        return [copies.start(ref.at[:, :, p.c], ref.at[:, :, p.c], p.partner)]

    wb_in = send_all(r.wb)
    vec_in = [
        copies.start(r.vec.at[p.c, pl.ds(chip, 1)], r.vec.at[p.c, pl.ds(chip, 1)], p.device(p.plane(a), p.corner(b)))
        for a, b in p.others()
    ]
    wh_in = send_all(r.wh_cut)
    up_in = send_planes(r.wu_cut)
    down_in = send_planes(r.wd)

    zero_sums(r)
    fill_pick(r, n, D, FF)
    loads[5].wait()
    run(enter, 0, nb)

    arrived(wb_in)
    wb_in = send_pair(r.wb)
    arrived(vec_in)
    vec_in = [copies.start(r.vec.at[p.c], r.vec.at[p.c], p.partner)]
    arrived(wb_in)
    arrived(vec_in)
    spread = mm_nt(r.vec[...].reshape(n, 128).astype(BF16), r.pick[...])
    vectors = jnp.sum(jnp.where(owners(n, D, FF), spread, 0.0), axis=0, keepdims=True)
    for name, lane, width, own, offset in segments(n, D, FF):
        getattr(r, name)[...] = vectors[:, lane : lane + width]

    run(backbone, 0, nb)
    arrived(wh_in)
    wh_in = send_pair(r.wh_cut)
    arrived(up_in)
    up_in = send_corners(r.wu_cut)
    arrived(down_in)
    down_in = send_corners(r.wd)
    arrived(wh_in)
    r.wh[...] = uncut(r.wh_cut[...].astype(F32)).reshape(D, 3 * D).astype(BF16)
    run(gates, 0, nb)
    arrived(up_in)
    up_in = send_pair(r.wu_cut)
    arrived(down_in)
    down_in = send_pair(r.wd)
    arrived(up_in)
    r.wu[...] = uncut(r.wu_cut[...].astype(F32)).reshape(D, FF).astype(BF16)
    arrived(down_in)
    loads[6].wait()
    run(feed_forward, 0, nb)
    outs = [pltpu.make_async_copy(r.out, r.out_hbm, r.local.at[7])]
    outs[0].start()

    up = Share(r, "u", cut, copies, p, False)
    down = Share(r, "d", same, copies, p, False)
    heads = Share(r, "h", cut, copies, p, True)
    back = Share(r, "b", same, copies, p, True)
    r.dwu[...] = mm_tn(r.normed[...], r.gpu[...]).reshape(r.dwu.shape)
    up.pair()
    r.dwd[...] = mm_tn(r.gout[...], r.hidden[...]).T.reshape(r.dwd.shape)
    down.pair()
    run(gates_back, 0, 1, True)
    up.spread()
    down.spread()
    run(gates_back, 1, nb - 1, True)
    up.climb()
    down.climb()
    run(gates_back, nb - 1, nb, True)
    r.dwh[...] = mm_tn(r.feat[...], r.gph[...]).reshape(r.dwh.shape)
    heads.pair()
    r.dwb[...] = mm_tn(r.gpb[...], r.joined[...]).T.reshape(r.dwb.shape)
    back.pair()

    sums = jnp.concatenate([jnp.sum(getattr(r, name)[...], axis=0, keepdims=True) for name in SUMS], axis=1)
    mine = owners(n, D, FF)
    rest, rows = jnp.where(mine, sums, 0.0), None
    for _ in range(3):
        part = rest.astype(BF16)
        rest = rest - part.astype(F32)
        row = mm(part, r.pick[...])
        rows = row if rows is None else rows + row
    r.vs[...] = rows.reshape(2, chips, 128)
    vec_pair = copies.start(r.vs.at[1 - p.c], r.vr, p.partner)
    run(leave, 0, 1, True)
    heads.spread()
    back.spread()
    vec_pair.wait_recv()
    r.va[...] = r.vs[p.c] + r.vr[...]
    vec_out = []
    for a, b in p.others():
        z, q = p.plane(a), p.corner(b)
        vec_out.append(copies.start(r.va.at[pl.ds(z * QUAD + q, 1)], r.vt.at[pl.ds(chip, 1)], p.device(z, q)))
    r.vt[pl.ds(chip, 1), :] = r.va[pl.ds(chip, 1), :]
    run(leave, 1, nb, True)
    outs.append(pltpu.make_async_copy(r.ig, r.ig_hbm, r.local.at[8]))
    outs[1].start()
    r.gup[...] = uncut(up.land())
    r.gdown[...] = down.land()
    r.gheads[...] = uncut(heads.land())
    r.gback[...] = back.land()
    arrived(vec_out)
    r.gvec[...] = jnp.sum(r.vt[...], axis=0, keepdims=True)
    copies.finish()
    for out in outs:
        out.wait()


def quick(lengths, x, cot, wb, wh, wu, wd, vectors, n):
    S = lengths.shape[0]
    T, D = x.shape
    L, FF = T // S, wu.shape[1]
    Z, chips, v = n // (2 * QUAD), n // 2, pltpu.VMEM
    space = work_space(S, L, D, FF)
    rb, rh, ru, rd = wb.shape[0], wh.shape[0], wu.shape[0], wd.shape[0]
    space.update(
        x=v((T, D), BF16), cot=v((T, D), BF16), out=v((T, D), BF16), ig=v((T, D), BF16),
        wb=v((Z, QUAD, 2, rb, D), BF16), wd=v((Z, QUAD, 2, rd, D), BF16),
        wh_cut=v((Z, QUAD, 2, 2 * rh, 3 * D // 2), BF16), wu_cut=v((Z, QUAD, 2, 2 * ru, FF // 2), BF16),
        wh=v((D, 3 * D), BF16), wu=v((D, FF), BF16), wh_mine=v((rh, 3 * D), BF16), wu_mine=v((ru, FF), BF16),
        vec=v((2, chips, 128), F32), pick=v((sum(sum_widths(D, FF)), 128), BF16),
        vs=v((2, chips, 128), F32), vr=v((chips, 128), F32), va=v((chips, 128), F32), vt=v((chips, 128), F32),
        local=pltpu.SemaphoreType.DMA((9,)), send=pltpu.SemaphoreType.DMA((160,)), recv=pltpu.SemaphoreType.DMA((160,)),
    )
    for name, lane, width, own, offset in segments(n, D, FF):
        space[name] = v((1, width), F32)
    space.update(share_space("u", n, ru, FF, True, False))
    space.update(share_space("d", n, rd, D, False, False))
    space.update(share_space("h", n, rh, 3 * D, True, True))
    space.update(share_space("b", n, rb, D, False, True))
    row = lambda a, b: jax.ShapeDtypeStruct((a, b), F32)
    shapes = (
        jax.ShapeDtypeStruct((T, D), BF16), jax.ShapeDtypeStruct((T, D), BF16),
        row(rb, D), row(rh, 3 * D), row(ru, FF), row(rd, D), row(1, 128),
    )
    hbm, vmem = pl.BlockSpec(memory_space=pl.ANY), pl.BlockSpec(memory_space=pltpu.VMEM)
    return pl.pallas_call(
        functools.partial(mega, INPUTS + OUTPUTS + tuple(space), (S, L, D), n, FF),
        out_shape=shapes,
        in_specs=[pl.BlockSpec(memory_space=pltpu.SMEM)] + [hbm] * 7,
        out_specs=[hbm, hbm] + [vmem] * 5,
        scratch_shapes=list(space.values()),
        compiler_params=pltpu.CompilerParams(collective_id=0, has_side_effects=True, vmem_limit_bytes=62 << 20),
    )(lengths, x, cot, wb, wh, wu, wd, vectors)


def plain(names, dims, *refs):
    r = refs_of(names, refs)
    S, L, D = dims
    nb = L // BLK

    def run(f, down=False):
        def step(i, c):
            f(nb - 1 - i if down else i, r, dims)
            return c
        lax.fori_loop(0, nb, step, 0)

    zero_sums(r)
    for f in (enter, backbone, gates, feed_forward):
        run(f)
    r.gup[...] = mm_tn(r.normed[...], r.gpu[...])
    r.gdown[...] = mm_tn(r.gout[...], r.hidden[...]).T
    run(gates_back, True)
    r.gheads[...] = mm_tn(r.feat[...], r.gph[...])
    r.gback[...] = mm_tn(r.gpb[...], r.joined[...]).T
    run(leave, True)
    for name in SUMS:
        getattr(r, "all" + name)[...] = jnp.sum(getattr(r, name)[...], axis=0, keepdims=True)


def whole(lengths, x, cot, matrices, vectors):
    S = lengths.shape[0]
    T, D = x.shape
    L, FF = T // S, matrices[2].shape[1]
    space = work_space(S, L, D, FF)
    names = ("lengths", "x", "cot", "wb", "wh", "wu", "wd", "bb", "bh", "g1", "b1", "g2", "b2", "bu", "bd")
    names += ("out", "ig") + ROWS[:4] + tuple("all" + name for name in SUMS) + tuple(space)
    row = lambda a, b: jax.ShapeDtypeStruct((a, b), F32)
    shapes = (jax.ShapeDtypeStruct((T, D), BF16),) * 2
    shapes += tuple(row(*m.shape) for m in matrices) + tuple(row(1, width) for width in sum_widths(D, FF))
    vmem = pl.BlockSpec(memory_space=pltpu.VMEM)
    return pl.pallas_call(
        functools.partial(plain, names, (S, L, D)),
        out_shape=shapes,
        in_specs=[pl.BlockSpec(memory_space=pltpu.SMEM)] + [vmem] * 14,
        out_specs=[vmem] * len(shapes),
        scratch_shapes=list(space.values()),
        compiler_params=pltpu.CompilerParams(vmem_limit_bytes=62 << 20),
    )(lengths, x, cot, *matrices, *(v.astype(F32).reshape(1, -1) for v in vectors))


def by_collectives(lengths, x, cot, matrices, vectors):
    gather = lambda a: lax.all_gather(a, "dp", axis=0, tiled=True)
    scatter = lambda a: lax.psum_scatter(a, "dp", scatter_dimension=0, tiled=True)
    results = whole(lengths, x, cot, [gather(m) for m in matrices], [gather(v) for v in vectors])
    return results[:2], [scatter(m) for m in results[2:6]], [scatter(v[0]) for v in results[6:]]


def by_kernel(lengths, x, cot, matrices, vectors, n):
    used = sum(v.shape[0] for v in vectors)
    row = jnp.concatenate(vectors + (jnp.zeros((128 - used,), BF16),)).astype(F32).reshape(1, 128)
    results = quick(lengths, x, cot, *matrices, row, n)
    pieces, at = [], 0
    for v in vectors:
        pieces.append(results[6][0, at : at + v.shape[0]])
        at += v.shape[0]
    return results[:2], results[2:6], pieces


def in_tiles(n, back_w, heads_w, up_w, down_w):
    rows = 2 * QUAD * down_w.shape[0]
    return (
        n % (2 * QUAD) == 0 and heads_w.shape[0] == 8 and up_w.shape[0] == 8
        and back_w.shape[0] % 16 == 0 and down_w.shape[0] % 16 == 0 and FF_STEP % rows == 0
    )


def local(n, block_in, lengths, back_w, back_b, heads_w, heads_b, norm1_gain, norm1_bias, norm2_gain, norm2_bias,
          up_w, up_b, down_w, down_b, cotangent):
    matrices = (back_w, heads_w, up_w, down_w)
    vectors = (back_b, heads_b, norm1_gain, norm1_bias, norm2_gain, norm2_bias, up_b, down_b)
    if in_tiles(n, *matrices):
        big, weights, small = by_kernel(lengths, block_in, cotangent, matrices, vectors, n)
    else:
        big, weights, small = by_collectives(lengths, block_in, cotangent, matrices, vectors)
    gback, gheads, gup, gdown = weights
    gb, gh, gg1, gb1, gg2, gb2, gu, gd = small
    return *big, gback, gb, gheads, gh, gg1, gb1, gg2, gb2, gup, gu, gdown, gd


def solution(mesh):
    n = mesh.shape["dp"]
    m, v = P("dp", None), P("dp")
    return jax.shard_map(
        functools.partial(local, n), mesh=mesh,
        in_specs=(m, v, m, v, m, v, v, v, v, v, m, v, m, v, m),
        out_specs=(m, m, m, v, m, v, v, v, v, v, m, v, m, v), check_vma=False,
    )
```

```python
import functools
import jax
import jax.numpy as jnp
from jax import lax
from jax.experimental import pallas as pl
from jax.experimental.pallas import tpu as pltpu
from jax.sharding import PartitionSpec as P

BLK = 256
LANES = 8
STEPS = BLK // LANES
QUAD = 4
FF_STEP = 256
F32 = jnp.float32
BF16 = jnp.bfloat16
MESH = pl.DeviceIdType.MESH
GC = 0.7978845608028654
GA = 0.044715


def mm(a, b):
    return lax.dot_general(a, b, (((1,), (0,)), ((), ())), preferred_element_type=F32)


def mm_nt(a, b):
    return lax.dot_general(a, b, (((1,), (1,)), ((), ())), preferred_element_type=F32)


def mm_tn(a, b):
    return lax.dot_general(a, b, (((0,), (0,)), ((), ())), preferred_element_type=F32)


def shuffle(transposed=False):
    row = lax.broadcasted_iota(jnp.int32, (BLK, BLK), 0)
    col = lax.broadcasted_iota(jnp.int32, (BLK, BLK), 1)
    if transposed:
        row, col = col, row
    return jnp.where((row & 7) * STEPS + (row >> 3) == col, 1.0, 0.0).astype(BF16)


def fold(values):
    return jnp.sum(values.reshape(values.shape[0] // 8, 8, values.shape[1]), axis=0)


def sublane(shape):
    return lax.broadcasted_iota(jnp.int32, shape, 0)


def flat(ref):
    values = ref[...]
    return values.reshape(-1, values.shape[-1])


def block_rows(i, dims):
    return pl.ds(i * (dims[0] * BLK), dims[0] * BLK)


def enter(i, r, dims):
    S, L, D = dims
    order = shuffle()
    sub = sublane((8, D))
    joined, cots = [], []
    for s in range(S):
        cots.append(mm(order, r.cot[pl.ds(s * L + i * BLK, BLK), :]))
        mixed = mm(order, r.x[pl.ds(s * L + i * BLK, BLK), :])
        turned = pltpu.roll(mixed[BLK - 8 :], 1, 0)
        first = jnp.where(sub == 0, jnp.where(i == 0, 0.0, r.xcarry[s]), turned)
        r.xcarry[s] = turned
        before = jnp.concatenate([first, mixed[: BLK - 8]], axis=0)
        joined.append(jnp.concatenate([mixed, before], axis=1))
    rows = block_rows(i, dims)
    r.joined[rows, :] = jnp.concatenate(joined, axis=0).astype(BF16)
    cot = jnp.concatenate(cots, axis=0)
    r.mixed_cot[rows, :] = cot.astype(BF16)
    gout = jnp.where(live(i, r, dims), cot, 0.0)
    r.gbd[...] += fold(gout)
    r.gout[rows, :] = gout.astype(BF16)


def backbone(i, r, dims):
    rows = block_rows(i, dims)
    inner = jnp.tanh(0.666 * (mm(r.joined[rows, :], flat(r.wb)) + r.bb[...]))
    r.inner[rows, :] = inner
    r.feat[rows, :] = (1.7159 * inner).astype(BF16)


def gates(i, r, dims):
    S, L, D = dims
    rows = block_rows(i, dims)
    sub = sublane((8, D))
    heads = mm(r.feat[rows, :], r.wh[...]) + r.bh[...]
    o = 0.5 * jnp.tanh(0.5 * heads[:, :D]) + 0.5
    v = jnp.tanh(heads[:, D : 2 * D])
    f = jnp.tanh(heads[:, 2 * D :])
    r.o[rows, :] = o
    r.v[rows, :] = v
    r.f[rows, :] = f
    keep = 1.0 - o
    drive = f + o * (v - f)
    one = jnp.ones((8, D), F32)
    for s in range(S):
        k = [keep[s * BLK + 8 * j : s * BLK + 8 * j + 8] for j in range(STEPS)]
        d = [drive[s * BLK + 8 * j : s * BLK + 8 * j + 8] for j in range(STEPS)]
        A, Q = k[0], d[0]
        for j in range(1, STEPS):
            Q = k[j] * Q + d[j]
            A = k[j] * A
        for sh in (1, 2, 4):
            An = jnp.where(sub < sh, one, pltpu.roll(A, sh, 0))
            Qn = jnp.where(sub < sh, 0.0, pltpu.roll(Q, sh, 0))
            Q = Q + A * Qn
            A = A * An
        carry = jnp.where(i == 0, 0.0, r.scarry[s])
        ends = Q + A * carry
        start = jnp.where(sub == 0, carry, pltpu.roll(ends, 1, 0))
        r.scarry[s] = jnp.broadcast_to(ends[7:8], (8, D))
        r.start[i, s] = start
        Q = start
        for j in range(STEPS):
            Q = k[j] * Q + d[j]
            r.state[pl.ds(i * (S * BLK) + s * BLK + 8 * j, 8), :] = Q


def live(i, r, dims):
    S, L, D = dims
    row = lax.broadcasted_iota(jnp.int32, (BLK, D), 0)
    time = (row & 7) * STEPS + (row >> 3) + i * BLK
    return jnp.concatenate([time < r.lengths[s] for s in range(S)], axis=0)


def normalise(values, D):
    mean = jnp.sum(values, axis=1, keepdims=True) * (1.0 / D)
    c = values - mean
    var = jnp.sum(c * c, axis=1, keepdims=True) * (1.0 / D)
    rs = lax.rsqrt(var + 1e-05)
    return c * rs, rs


def norm_back(dy, gain, xhat, rs, D):
    dx = dy * gain
    m1 = jnp.sum(dx, axis=1, keepdims=True) * (1.0 / D)
    m2 = jnp.sum(dx * xhat, axis=1, keepdims=True) * (1.0 / D)
    return rs * (dx - m1 - xhat * m2)


def feed_forward(i, r, dims):
    S, L, D = dims
    FF = r.wu.shape[1]
    rows = block_rows(i, dims)
    valid = live(i, r, dims)
    g1, b1, g2, b2 = r.g1[...], r.b1[...], r.g2[...], r.b2[...]
    xhat1, rs1 = normalise(r.state[rows, :], D)
    mid = r.joined[rows, pl.ds(0, D)].astype(F32) + jnp.where(valid, xhat1 * g1 + b1, 0.0)
    xhat2, rs2 = normalise(mid, D)
    normed = (xhat2 * g2 + b2).astype(BF16)
    r.normed[rows, :] = normed
    r.mid[rows, :] = mid
    gout = r.gout[rows, :]
    W = FF_STEP
    gn = None
    for n in range(FF // W):
        cols = slice(n * W, (n + 1) * W)
        down = r.wd_rows(n, W)
        pu = mm(normed, r.wu[:, cols]) + r.bu[:, cols]
        v2 = pu * pu
        h = 0.5 * jnp.tanh(pu * (v2 * (GC * GA) + GC)) + 0.5
        hid = pu * h
        r.hidden[rows, cols] = hid.astype(BF16)
        slope = h + hid * (1.0 - h) * (v2 * (6.0 * GA * GC) + 2.0 * GC)
        gpu = (mm_nt(gout, down) * slope).astype(BF16)
        r.gpu[rows, cols] = gpu
        r.gbu[:, cols] += fold(gpu.astype(F32))
        gnn = mm_nt(gpu, r.wu[:, cols])
        gn = gnn if gn is None else gn + gnn
    r.gg2[...] += fold(gn * xhat2)
    r.gb2[...] += fold(gn)
    gmid = r.mixed_cot[rows, :].astype(F32) + norm_back(gn, g2, xhat2, rs2, D)
    r.gmid[rows, :] = gmid
    dy1 = jnp.where(valid, gmid, 0.0)
    r.gg1[...] += fold(dy1 * xhat1)
    r.gb1[...] += fold(dy1)
    r.gnorm[rows, :] = norm_back(dy1, g1, xhat1, rs1, D)


def gates_back(i, r, dims):
    S, L, D = dims
    nb = L // BLK
    rows = block_rows(i, dims)
    sub = sublane((8, D))
    o = r.o[rows, :]
    keep = 1.0 - o
    gnorm = r.gnorm[rows, :]
    state = r.state[rows, :]
    gss, sps = [], []
    one = jnp.ones((8, D), F32)
    for s in range(S):
        k = [keep[s * BLK + 8 * j : s * BLK + 8 * j + 8] for j in range(STEPS)]
        g = [gnorm[s * BLK + 8 * j : s * BLK + 8 * j + 8] for j in range(STEPS)]
        A = k[STEPS - 1]
        H = k[STEPS - 1] * g[STEPS - 1]
        for j in range(STEPS - 2, -1, -1):
            H = k[j] * (g[j] + H)
            A = k[j] * A
        for sh in (1, 2, 4):
            An = jnp.where(sub >= 8 - sh, one, pltpu.roll(A, 8 - sh, 0))
            Hn = jnp.where(sub >= 8 - sh, 0.0, pltpu.roll(H, 8 - sh, 0))
            H = H + A * Hn
            A = A * An
        carry = jnp.where(i == nb - 1, 0.0, r.scarry[s])
        ends = H + A * carry
        r.scarry[s] = jnp.broadcast_to(ends[0:1], (8, D))
        H = jnp.where(sub == 7, carry, pltpu.roll(ends, 7, 0))
        out = [None] * STEPS
        for j in range(STEPS - 1, -1, -1):
            G = g[j] + H
            H = k[j] * G
            out[j] = G
        gss += out
        sps += [r.start[i, s], state[s * BLK : (s + 1) * BLK - 8]]
    gs = jnp.concatenate(gss, axis=0)
    sp = jnp.concatenate(sps, axis=0)
    v = r.v[rows, :]
    f = r.f[rows, :]
    go = gs * o
    grate = go * keep * (v - f - sp)
    gv = go * (1.0 - v * v)
    gf = (gs - go) * (1.0 - f * f)
    gph = jnp.concatenate([grate, gv, gf], axis=1).astype(BF16)
    r.gph[rows, :] = gph
    r.gbh[...] += fold(gph.astype(F32))
    inner = r.inner[rows, :]
    gpb = (mm_nt(gph, r.wh[...]) * ((1.7159 * 0.666) * (1.0 - inner * inner))).astype(BF16)
    r.gpb[rows, :] = gpb
    r.gbb[...] += fold(gpb.astype(F32))


def emit(i, r, dims):
    S, L, D = dims
    rows = block_rows(i, dims)
    back = shuffle(True)
    branch = mm(r.hidden[rows, :], flat(r.wd)) + r.bd[...]
    out = (r.mid[rows, :] + jnp.where(live(i, r, dims), branch, 0.0)).astype(BF16)
    for s in range(S):
        r.out[pl.ds(s * L + i * BLK, BLK), :] = mm(back, out[s * BLK : (s + 1) * BLK]).astype(BF16)


def leave(i, r, dims):
    S, L, D = dims
    nb = L // BLK
    rows = block_rows(i, dims)
    sub = sublane((8, D))
    back = shuffle(True)
    gj = mm_nt(r.gpb[rows, :], flat(r.wb))
    gmid = r.gmid[rows, :]
    for s in range(S):
        own = gj[s * BLK : (s + 1) * BLK, :D]
        before = gj[s * BLK : (s + 1) * BLK, D:]
        turned = pltpu.roll(before[:8], 7, 0)
        last = jnp.where(sub == 7, jnp.where(i == nb - 1, 0.0, r.xcarry[s]), turned)
        r.xcarry[s] = turned
        moved = jnp.concatenate([before[8:], last], axis=0)
        grad = (gmid[s * BLK : (s + 1) * BLK] + own + moved).astype(BF16)
        r.ig[pl.ds(s * L + i * BLK, BLK), :] = mm(back, grad).astype(BF16)


SUMS = ("gbb", "gbh", "gg1", "gb1", "gg2", "gb2", "gbu", "gbd")


def zero_sums(r):
    for name in SUMS:
        ref = getattr(r, name)
        ref[...] = jnp.zeros_like(ref)


def sum_widths(D, FF):
    return (D, 3 * D, D, D, D, D, FF, D)


def work_space(S, L, D, FF):
    T = S * L
    v = pltpu.VMEM
    space = dict(
        joined=v((T, 2 * D), BF16), inner=v((T, D), F32), feat=v((T, D), BF16),
        o=v((T, D), F32), v=v((T, D), F32), f=v((T, D), F32), state=v((T, D), F32),
        start=v((L // BLK, S, 8, D), F32), xcarry=v((S, 8, D), F32), scarry=v((S, 8, D), F32),
        normed=v((T, D), BF16), gout=v((T, D), BF16), hidden=v((T, FF), BF16), gpu=v((T, FF), BF16),
        mixed_cot=v((T, D), BF16), mid=v((T, D), F32), gmid=v((T, D), F32), gnorm=v((T, D), F32), gph=v((T, 3 * D), BF16), gpb=v((T, D), BF16),
    )
    for name, width in zip(SUMS, sum_widths(D, FF)):
        space[name] = v((8, width), F32)
    return space


class Refs:
    def wd_rows(self, n, width):
        if len(self.wd.shape) == 2:
            return self.wd[pl.ds(n * width, width), :]
        z, q, c, piece, columns = self.wd.shape
        plane = q * c * piece
        return self.wd[pl.ds(n * width // plane, width // plane)].reshape(width, columns)


def refs_of(names, refs):
    r = Refs()
    for name, ref in zip(names, refs):
        setattr(r, name, ref)
    return r


class Place:
    def __init__(self, n):
        self.n = n
        self.planes = n // (2 * QUAD)
        self.me = lax.axis_index("dp")
        self.c = self.me % 2
        self.q = (self.me // 2) % QUAD
        self.z = self.me // (2 * QUAD)
        self.partner = self.me + 1 - 2 * self.c

    def plane(self, k):
        return (self.z + k) % self.planes

    def corner(self, k):
        return (self.q + k) % QUAD

    def device(self, z, q):
        return (z * QUAD + q) * 2 + self.c

    def peers(self):
        found = [self.device(self.plane(a), self.q) for a in range(1, self.planes)]
        found += [self.device(self.z, self.corner(b)) for b in range(1, QUAD)]
        return found + [self.partner]


class Copies:
    def __init__(self, send, recv):
        self.send, self.recv, self.used, self.open = send, recv, 0, []

    def start(self, src, dst, device):
        k = self.used
        self.used += 1
        copy = pltpu.make_async_remote_copy(
            src_ref=src, dst_ref=dst, send_sem=self.send.at[k], recv_sem=self.recv.at[k],
            device_id=(device,), device_id_type=MESH,
        )
        copy.start()
        self.open.append(copy)
        return copy

    def finish(self):
        for copy in self.open:
            copy.wait_send()


def arrived(copies):
    for copy in copies:
        copy.wait_recv()


def cut(values):
    half = values.shape[-1] // 2
    return jnp.concatenate([values[..., :half], values[..., half:]], axis=-2)


def uncut(values):
    return jnp.concatenate([values[..., :8, :], values[..., 8:, :]], axis=-1)


def same(values):
    return values


class Share:
    def __init__(self, r, name, cutter, copies, place):
        self.r, self.name, self.cut, self.copies, self.p = r, name, cutter, copies, place

    def ref(self, kind):
        return getattr(self.r, kind + self.name)

    def pair(self):
        p = self.p
        self.ref("cs")[...] = self.cut(self.ref("dw")[:, :, 1 - p.c]).astype(BF16)
        self.sent = [self.copies.start(self.ref("cs"), self.ref("cr"), p.partner)]

    def spread(self):
        p = self.p
        arrived(self.sent)
        total = self.cut(self.ref("dw")[:, :, p.c]) + self.ref("cr")[...].astype(F32)
        self.ref("xs")[...] = total.astype(BF16)
        self.sent = []
        for b in range(1, QUAD):
            q = p.corner(b)
            self.sent.append(self.copies.start(self.ref("xs").at[:, q], self.ref("xr").at[b - 1], p.device(p.z, q)))

    def climb(self):
        p = self.p
        arrived(self.sent)
        total = self.cut(self.ref("dw")[:, p.q, p.c]) + self.ref("cr")[:, p.q].astype(F32)
        for b in range(QUAD - 1):
            total = total + self.ref("xr")[b].astype(F32)
        self.ref("ac")[...] = total
        self.ref("zs")[...] = total.astype(BF16)
        self.sent = []
        for a in range(1, p.planes):
            z = p.plane(a)
            self.sent.append(self.copies.start(self.ref("zs").at[z], self.ref("zr").at[a - 1], p.device(z, p.q)))

    def land(self):
        arrived(self.sent)
        total = self.ref("ac")[self.p.z]
        for k in range(self.p.planes - 1):
            total = total + self.ref("zr")[k].astype(F32)
        return total


def share_space(name, n, rows, columns, cutting):
    Z, v = n // (2 * QUAD), pltpu.VMEM
    R, C = (2 * rows, columns // 2) if cutting else (rows, columns)
    return {
        "dw" + name: v((Z, QUAD, 2, rows, columns), F32),
        "cs" + name: v((Z, QUAD, R, C), BF16),
        "cr" + name: v((Z, QUAD, R, C), BF16),
        "xs" + name: v((Z, QUAD, R, C), BF16),
        "xr" + name: v((QUAD - 1, Z, R, C), BF16),
        "ac" + name: v((Z, R, C), F32),
        "zs" + name: v((Z, R, C), BF16),
        "zr" + name: v((Z - 1, R, C), BF16),
    }


def segments(n, D, FF):
    found, lane, offset = [], 0, 0
    for name, width in zip(("bb", "bh", "g1", "b1", "g2", "b2", "bu", "bd"), sum_widths(D, FF)):
        found.append((name, lane, width, width // n, offset))
        lane, offset = lane + width, offset + width // n
    return found


def fill_pick(r, n, D, FF):
    for name, lane, width, own, offset in segments(n, D, FF):
        l = lax.broadcasted_iota(jnp.int32, (width, 128), 0).astype(F32)
        k = lax.broadcasted_iota(jnp.int32, (width, 128), 1).astype(F32)
        place = l - own * jnp.floor((l + 0.5) * (1.0 / own)) + offset
        r.pick[pl.ds(lane, width), :] = jnp.where(place == k, 1.0, 0.0).astype(BF16)


def owners(n, D, FF):
    parts, Z = [], n // (2 * QUAD)
    for name, lane, width, own, offset in segments(n, D, FF):
        l = lax.broadcasted_iota(jnp.int32, (n, width), 1).astype(F32)
        row = lax.broadcasted_iota(jnp.int32, (n, width), 0)
        z, q, c = row % Z, row // Z % QUAD, row // (Z * QUAD)
        device = ((z * QUAD + q) * 2 + c).astype(F32)
        parts.append(jnp.floor((l + 0.5) * (1.0 / own)) == device)
    return jnp.concatenate(parts, axis=1)


ROWS = ("gback", "gheads", "gup", "gdown", "gvec")
INPUTS = ("lengths", "x_hbm", "cot_hbm", "wb_own", "wh_own", "wu_own", "wd_own", "vec_own")
OUTPUTS = ("out_hbm", "ig_hbm") + ROWS


def mega(names, dims, n, FF, *refs):
    r = refs_of(names, refs)
    S, L, D = dims
    nb = L // BLK
    p = Place(n)
    copies = Copies(r.send, r.recv)

    def run(f, first, last, down=False):
        def step(i, c):
            f(nb - 1 - i if down else i, r, dims)
            return c
        lax.fori_loop(first, last, step, 0)

    barrier = pltpu.get_barrier_semaphore()
    for peer in p.peers():
        pl.semaphore_signal(barrier, inc=1, device_id=(peer,), device_id_type=MESH)

    loads = [
        pltpu.make_async_copy(src, dst, r.local.at[k])
        for k, (src, dst) in enumerate((
            (r.wb_own, r.wb.at[p.z, p.q, p.c]), (r.vec_own, r.vec.at[p.c, p.q, pl.ds(p.z, 1)]),
            (r.wh_own, r.wh_mine), (r.wu_own, r.wu_mine), (r.wd_own, r.wd.at[p.z, p.q, p.c]),
            (r.x_hbm, r.x), (r.cot_hbm, r.cot),
        ))
    ]
    for load in loads:
        load.start()
    for load in loads[:5]:
        load.wait()
    r.wh_cut[p.z, p.q, p.c] = cut(r.wh_mine[...].astype(F32)).astype(BF16)
    r.wu_cut[p.z, p.q, p.c] = cut(r.wu_mine[...].astype(F32)).astype(BF16)
    pl.semaphore_wait(barrier, len(p.peers()))

    def to_planes(own):
        return [copies.start(own, own, p.device(p.plane(a), p.q)) for a in range(1, p.planes)]

    def to_corners(own):
        return [copies.start(own, own, p.device(p.z, p.corner(b))) for b in range(1, QUAD)]

    def to_partner(own):
        return [copies.start(own, own, p.partner)]

    weights = (r.wb, r.wh_cut, r.wu_cut, r.wd)
    wb_in = to_planes(r.wb.at[p.z, p.q, p.c])
    vec_in = to_planes(r.vec.at[p.c, p.q, pl.ds(p.z, 1)])
    wh_in, up_in, down_in = (to_planes(ref.at[p.z, p.q, p.c]) for ref in weights[1:])

    zero_sums(r)
    arrived(wb_in)
    wb_in = to_corners(r.wb.at[:, p.q, p.c])
    arrived(vec_in)
    vec_in = to_corners(r.vec.at[p.c, p.q])
    arrived(wh_in)
    wh_in = to_corners(r.wh_cut.at[:, p.q, p.c])
    loads[5].wait()
    loads[6].wait()
    run(enter, 0, nb)
    fill_pick(r, n, D, FF)
    arrived(wb_in)
    wb_in = to_partner(r.wb.at[:, :, p.c])
    arrived(vec_in)
    vec_in = to_partner(r.vec.at[p.c])
    arrived(up_in)
    up_in = to_corners(r.wu_cut.at[:, p.q, p.c])
    arrived(down_in)
    down_in = to_corners(r.wd.at[:, p.q, p.c])
    arrived(wb_in)
    arrived(vec_in)
    spread = mm_nt(r.vec[...].reshape(n, 128).astype(BF16), r.pick[...])
    vectors = jnp.sum(jnp.where(owners(n, D, FF), spread, 0.0), axis=0, keepdims=True)
    for name, lane, width, own, offset in segments(n, D, FF):
        getattr(r, name)[...] = vectors[:, lane : lane + width]

    arrived(wh_in)
    wh_in = to_partner(r.wh_cut.at[:, :, p.c])
    run(backbone, 0, nb)
    arrived(wh_in)
    r.wh[...] = uncut(r.wh_cut[...].astype(F32)).reshape(D, 3 * D).astype(BF16)
    run(gates, 0, nb)
    arrived(up_in)
    up_in = to_partner(r.wu_cut.at[:, :, p.c])
    arrived(down_in)
    down_in = to_partner(r.wd.at[:, :, p.c])
    arrived(up_in)
    r.wu[...] = uncut(r.wu_cut[...].astype(F32)).reshape(D, FF).astype(BF16)
    arrived(down_in)
    run(feed_forward, 0, nb)

    up = Share(r, "u", cut, copies, p)
    down = Share(r, "d", same, copies, p)
    heads = Share(r, "h", cut, copies, p)
    back = Share(r, "b", same, copies, p)
    r.dwu[...] = mm_tn(r.normed[...], r.gpu[...]).reshape(r.dwu.shape)
    up.pair()
    r.dwd[...] = mm_tn(r.gout[...], r.hidden[...]).T.reshape(r.dwd.shape)
    down.pair()
    run(gates_back, 0, 1, True)
    up.spread()
    down.spread()
    run(gates_back, 1, nb, True)
    r.dwh[...] = mm_tn(r.feat[...], r.gph[...]).reshape(r.dwh.shape)
    heads.pair()
    r.dwb[...] = mm_tn(r.gpb[...], r.joined[...]).T.reshape(r.dwb.shape)
    back.pair()

    sums = jnp.concatenate([jnp.sum(getattr(r, name)[...], axis=0, keepdims=True) for name in SUMS], axis=1)
    rest, rows = jnp.where(owners(n, D, FF), sums, 0.0), None
    for _ in range(3):
        part = rest.astype(BF16)
        rest = rest - part.astype(F32)
        row = mm(part, r.pick[...])
        rows = row if rows is None else rows + row
    r.vs[...] = rows.reshape(r.vs.shape)
    vec_out = [copies.start(r.vs.at[1 - p.c], r.vr, p.partner)]
    heads.spread()
    back.spread()
    arrived(vec_out)
    r.va[...] = r.vs[p.c] + r.vr[...]
    vec_out = []
    for b in range(1, QUAD):
        q = p.corner(b)
        vec_out.append(copies.start(r.va.at[q], r.vx.at[b - 1], p.device(p.z, q)))
    up.climb()
    down.climb()
    run(leave, 0, nb, True)
    outs = [pltpu.make_async_copy(r.ig, r.ig_hbm, r.local.at[7])]
    outs[0].start()
    heads.climb()
    back.climb()
    arrived(vec_out)
    total = r.va[p.q]
    for b in range(QUAD - 1):
        total = total + r.vx[b]
    r.vz[...] = total
    vec_out = []
    for a in range(1, p.planes):
        z = p.plane(a)
        vec_out.append(copies.start(r.vz.at[pl.ds(z, 1)], r.vt.at[pl.ds(a - 1, 1)], p.device(z, p.q)))
    run(emit, 0, nb)
    outs.append(pltpu.make_async_copy(r.out, r.out_hbm, r.local.at[8]))
    outs[1].start()
    r.gup[...] = uncut(up.land())
    r.gdown[...] = down.land()
    r.gheads[...] = uncut(heads.land())
    r.gback[...] = back.land()
    arrived(vec_out)
    r.gvec[...] = r.vz[pl.ds(p.z, 1), :] + jnp.sum(r.vt[...], axis=0, keepdims=True)
    copies.finish()
    for out in outs:
        out.wait()


def quick(lengths, x, cot, wb, wh, wu, wd, vectors, n):
    S = lengths.shape[0]
    T, D = x.shape
    L, FF = T // S, wu.shape[1]
    Z, v = n // (2 * QUAD), pltpu.VMEM
    space = work_space(S, L, D, FF)
    rb, rh, ru, rd = wb.shape[0], wh.shape[0], wu.shape[0], wd.shape[0]
    space.update(
        x=v((T, D), BF16), cot=v((T, D), BF16), out=v((T, D), BF16), ig=v((T, D), BF16),
        wb=v((Z, QUAD, 2, rb, D), BF16), wd=v((Z, QUAD, 2, rd, D), BF16),
        wh_cut=v((Z, QUAD, 2, 2 * rh, 3 * D // 2), BF16), wu_cut=v((Z, QUAD, 2, 2 * ru, FF // 2), BF16),
        wh=v((D, 3 * D), BF16), wu=v((D, FF), BF16), wh_mine=v((rh, 3 * D), BF16), wu_mine=v((ru, FF), BF16),
        vec=v((2, QUAD, Z, 128), F32), pick=v((sum(sum_widths(D, FF)), 128), BF16),
        vs=v((2, QUAD, Z, 128), F32), vr=v((QUAD, Z, 128), F32), va=v((QUAD, Z, 128), F32),
        vx=v((QUAD - 1, Z, 128), F32), vz=v((Z, 128), F32), vt=v((Z - 1, 128), F32),
        local=pltpu.SemaphoreType.DMA((9,)), send=pltpu.SemaphoreType.DMA((72,)), recv=pltpu.SemaphoreType.DMA((72,)),
    )
    for name, lane, width, own, offset in segments(n, D, FF):
        space[name] = v((1, width), F32)
    space.update(share_space("u", n, ru, FF, True))
    space.update(share_space("d", n, rd, D, False))
    space.update(share_space("h", n, rh, 3 * D, True))
    space.update(share_space("b", n, rb, D, False))
    row = lambda a, b: jax.ShapeDtypeStruct((a, b), F32)
    shapes = (
        jax.ShapeDtypeStruct((T, D), BF16), jax.ShapeDtypeStruct((T, D), BF16),
        row(rb, D), row(rh, 3 * D), row(ru, FF), row(rd, D), row(1, 128),
    )
    hbm, vmem = pl.BlockSpec(memory_space=pl.ANY), pl.BlockSpec(memory_space=pltpu.VMEM)
    results = pl.pallas_call(
        functools.partial(mega, INPUTS + OUTPUTS + tuple(space), (S, L, D), n, FF),
        out_shape=shapes,
        in_specs=[pl.BlockSpec(memory_space=pltpu.SMEM)] + [hbm] * 7,
        out_specs=[hbm] * 2 + [vmem] * 5,
        scratch_shapes=list(space.values()),
        compiler_params=pltpu.CompilerParams(collective_id=0, has_side_effects=True, vmem_limit_bytes=62 << 20),
    )(lengths, x, cot, wb, wh, wu, wd, vectors)
    return hand_over(results, [own for name, lane, width, own, offset in segments(n, D, FF)])


def hand_over_kernel(widths, parts, *refs):
    count = len(parts)
    sources, targets = refs[: count + 1], refs[count + 1 : 2 * count + 1]
    smalls = refs[2 * count + 1 : 2 * count + 1 + len(widths)]
    stages, sem_in, sem_out = refs[-count - 3 : -2], refs[-2], refs[-1]
    moves, k = [], 0
    for source, stage, cuts in zip(sources, stages, (1,) + parts):
        rows = source.shape[0] // cuts
        for j in range(cuts):
            piece = pl.ds(j * rows, rows)
            move = pltpu.make_async_copy(source.at[piece], stage.at[piece], sem_in.at[k])
            move.start()
            moves.append((move, stage.at[piece], piece))
            k += 1
    moves[0][0].wait()
    at = 0
    for small, width in zip(smalls, widths):
        small[...] = pltpu.roll(stages[0][...], (128 - at) % 128, 1)[:, :width]
        at += width
    k, out = 1, []
    for target, cuts in zip(targets, parts):
        for j in range(cuts):
            move, stage, piece = moves[k]
            move.wait()
            out.append(pltpu.make_async_copy(stage, target.at[piece], sem_out.at[k - 1]))
            out[-1].start()
            k += 1
    for move in out:
        move.wait()


def hand_over(results, widths):
    hbm, vmem = pl.BlockSpec(memory_space=pl.ANY), pl.BlockSpec(memory_space=pltpu.VMEM)
    results = results[6:] + results[:6]
    parts = (4, 4, 1, 1, 1, 1)
    shapes = [jax.ShapeDtypeStruct(a.shape, a.dtype) for a in results[1:]]
    shapes += [jax.ShapeDtypeStruct((1, w), F32) for w in widths]
    return pl.pallas_call(
        functools.partial(hand_over_kernel, widths, parts),
        out_shape=shapes,
        in_specs=[hbm] * len(results),
        out_specs=[hbm] * len(parts) + [vmem] * len(widths),
        scratch_shapes=[pltpu.VMEM(a.shape, a.dtype) for a in results]
        + [pltpu.SemaphoreType.DMA((sum(parts) + 1,)), pltpu.SemaphoreType.DMA((sum(parts),))],
        compiler_params=pltpu.CompilerParams(vmem_limit_bytes=62 << 20),
    )(*results)


def plain(names, dims, *refs):
    r = refs_of(names, refs)
    S, L, D = dims
    nb = L // BLK

    def run(f, down=False):
        def step(i, c):
            f(nb - 1 - i if down else i, r, dims)
            return c
        lax.fori_loop(0, nb, step, 0)

    zero_sums(r)
    for f in (enter, backbone, gates, feed_forward):
        run(f)
    r.gup[...] = mm_tn(r.normed[...], r.gpu[...])
    r.gdown[...] = mm_tn(r.gout[...], r.hidden[...]).T
    run(emit)
    run(gates_back, True)
    r.gheads[...] = mm_tn(r.feat[...], r.gph[...])
    r.gback[...] = mm_tn(r.gpb[...], r.joined[...]).T
    run(leave, True)
    for name in SUMS:
        getattr(r, "all" + name)[...] = jnp.sum(getattr(r, name)[...], axis=0, keepdims=True)


def whole(lengths, x, cot, matrices, vectors):
    S = lengths.shape[0]
    T, D = x.shape
    L, FF = T // S, matrices[2].shape[1]
    space = work_space(S, L, D, FF)
    names = ("lengths", "x", "cot", "wb", "wh", "wu", "wd", "bb", "bh", "g1", "b1", "g2", "b2", "bu", "bd")
    names += ("out", "ig") + ROWS[:4] + tuple("all" + name for name in SUMS) + tuple(space)
    row = lambda a, b: jax.ShapeDtypeStruct((a, b), F32)
    shapes = (jax.ShapeDtypeStruct((T, D), BF16),) * 2
    shapes += tuple(row(*m.shape) for m in matrices) + tuple(row(1, width) for width in sum_widths(D, FF))
    vmem = pl.BlockSpec(memory_space=pltpu.VMEM)
    return pl.pallas_call(
        functools.partial(plain, names, (S, L, D)),
        out_shape=shapes,
        in_specs=[pl.BlockSpec(memory_space=pltpu.SMEM)] + [vmem] * 14,
        out_specs=[vmem] * len(shapes),
        scratch_shapes=list(space.values()),
        compiler_params=pltpu.CompilerParams(vmem_limit_bytes=62 << 20),
    )(lengths, x, cot, *matrices, *(v.astype(F32).reshape(1, -1) for v in vectors))


def by_collectives(lengths, x, cot, matrices, vectors):
    gather = lambda a: lax.all_gather(a, "dp", axis=0, tiled=True)
    scatter = lambda a: lax.psum_scatter(a, "dp", scatter_dimension=0, tiled=True)
    results = whole(lengths, x, cot, [gather(m) for m in matrices], [gather(v) for v in vectors])
    return results[:2], [scatter(m) for m in results[2:6]], [scatter(v[0]) for v in results[6:]]


def by_kernel(lengths, x, cot, matrices, vectors, n):
    used = sum(v.shape[0] for v in vectors)
    row = jnp.concatenate(vectors + (jnp.zeros((128 - used,), BF16),)).astype(F32).reshape(1, 128)
    results = quick(lengths, x, cot, *matrices, row, n)
    return results[:2], results[2:6], [row[0] for row in results[6:]]


def in_tiles(n, back_w, heads_w, up_w, down_w):
    rows = 2 * QUAD * down_w.shape[0]
    return (
        n % (2 * QUAD) == 0 and heads_w.shape[0] == 8 and up_w.shape[0] == 8
        and back_w.shape[0] % 16 == 0 and down_w.shape[0] % 16 == 0 and FF_STEP % rows == 0
    )


def local(n, block_in, lengths, back_w, back_b, heads_w, heads_b, norm1_gain, norm1_bias, norm2_gain, norm2_bias,
          up_w, up_b, down_w, down_b, cotangent):
    matrices = (back_w, heads_w, up_w, down_w)
    vectors = (back_b, heads_b, norm1_gain, norm1_bias, norm2_gain, norm2_bias, up_b, down_b)
    if in_tiles(n, *matrices):
        big, weights, small = by_kernel(lengths, block_in, cotangent, matrices, vectors, n)
    else:
        big, weights, small = by_collectives(lengths, block_in, cotangent, matrices, vectors)
    gback, gheads, gup, gdown = weights
    gb, gh, gg1, gb1, gg2, gb2, gu, gd = small
    return *big, gback, gb, gheads, gh, gg1, gb1, gg2, gb2, gup, gu, gdown, gd


def solution(mesh):
    n = mesh.shape["dp"]
    m, v = P("dp", None), P("dp")
    return jax.shard_map(
        functools.partial(local, n), mesh=mesh,
        in_specs=(m, v, m, v, m, v, v, v, v, v, m, v, m, v, m),
        out_specs=(m, m, m, v, m, v, v, v, v, v, m, v, m, v), check_vma=False,
    )
```

```python
import functools
import jax
import jax.numpy as jnp
from jax import lax
from jax.experimental import pallas as pl
from jax.experimental.pallas import tpu as pltpu
from jax.sharding import PartitionSpec as P

BLK = 256
LANES = 8
STEPS = BLK // LANES
QUAD = 4
FF_STEP = 256
UP_PLANE, DOWN_PLANE, HEADS_PLANE, BACK_PLANE = False, False, False, True
F32 = jnp.float32
BF16 = jnp.bfloat16
MESH = pl.DeviceIdType.MESH
GC = 0.7978845608028654
GA = 0.044715


def mm(a, b):
    return lax.dot_general(a, b, (((1,), (0,)), ((), ())), preferred_element_type=F32)


def mm_nt(a, b):
    return lax.dot_general(a, b, (((1,), (1,)), ((), ())), preferred_element_type=F32)


def mm_tn(a, b):
    return lax.dot_general(a, b, (((0,), (0,)), ((), ())), preferred_element_type=F32)


def shuffle(transposed=False):
    row = lax.broadcasted_iota(jnp.int32, (BLK, BLK), 0)
    col = lax.broadcasted_iota(jnp.int32, (BLK, BLK), 1)
    if transposed:
        row, col = col, row
    return jnp.where((row & 7) * STEPS + (row >> 3) == col, 1.0, 0.0).astype(BF16)


def fold(values):
    return jnp.sum(values.reshape(values.shape[0] // 8, 8, values.shape[1]), axis=0)


def sublane(shape):
    return lax.broadcasted_iota(jnp.int32, shape, 0)


def flat(ref):
    values = ref[...]
    return values.reshape(-1, values.shape[-1])


def block_rows(i, dims):
    return pl.ds(pl.multiple_of(i * (dims[0] * BLK), dims[0] * BLK), dims[0] * BLK)


def add_to(ref, columns, values):
    ref[..., columns] += values.reshape(ref.shape[:-1] + values.shape[-1:])


def live(i, r, dims):
    S, L, D = dims
    row = lax.broadcasted_iota(jnp.int32, (BLK, D), 0)
    time = (row & 7) * STEPS + (row >> 3) + i * BLK
    return jnp.concatenate([time < r.lengths[s] for s in range(S)], axis=0)


def enter(i, r, dims):
    S, L, D = dims
    order = shuffle()
    sub = sublane((8, D))
    joined, cots = [], []
    for s in range(S):
        cots.append(mm(order, r.cot[pl.ds(s * L + i * BLK, BLK), :]))
        mixed = mm(order, r.x[pl.ds(s * L + i * BLK, BLK), :])
        turned = pltpu.roll(mixed[BLK - 8 :], 1, 0)
        first = jnp.where(sub == 0, jnp.where(i == 0, 0.0, r.xcarry[s]), turned)
        r.xcarry[s] = turned
        before = jnp.concatenate([first, mixed[: BLK - 8]], axis=0)
        joined.append(jnp.concatenate([mixed, before], axis=1))
    rows = block_rows(i, dims)
    joined = jnp.concatenate(joined, axis=0).astype(BF16)
    r.joined[rows, :] = joined
    r.joined_t[pl.ds(0, 2 * D), rows] = joined.T
    cot = jnp.concatenate(cots, axis=0)
    r.mixed_cot[rows, :] = cot.astype(BF16)
    gout = jnp.where(live(i, r, dims), cot, 0.0)
    r.gbd[...] += fold(gout)
    half = (0.5 * gout).astype(BF16)
    r.half[rows, :] = half
    r.half_t[:, rows] = half.T


def backbone(i, r, dims):
    S, L, D = dims
    rows = block_rows(i, dims)
    inner = jnp.tanh(0.666 * (mm(r.joined[rows, :], flat(r.wb)) + r.bb[...]))
    r.bend[rows, :] = (1.7159 * 0.666) * (1.0 - inner * inner)
    feat = (1.7159 * inner).astype(BF16)
    r.feat[rows, :] = feat
    r.feat_t[pl.ds(0, D), rows] = feat.T


def gates(i, r, dims):
    S, L, D = dims
    rows = block_rows(i, dims)
    sub = sublane((8, D))
    heads = mm(r.feat[rows, :], r.wh[...]) + r.bh[...]
    o = 0.5 * jnp.tanh(0.5 * heads[:, :D]) + 0.5
    v = jnp.tanh(heads[:, D : 2 * D])
    f = jnp.tanh(heads[:, 2 * D :])
    keep = 1.0 - o
    gap = v - f
    drive = f + o * gap
    r.keep[rows, :] = keep
    r.to_value[rows, :] = o * (1.0 - v * v)
    r.to_fallback[rows, :] = keep * (1.0 - f * f)
    bend = o * keep
    one = jnp.ones((8, D), F32)
    for s in range(S):
        k = [keep[s * BLK + 8 * j : s * BLK + 8 * j + 8] for j in range(STEPS)]
        d = [drive[s * BLK + 8 * j : s * BLK + 8 * j + 8] for j in range(STEPS)]
        A, Q = k[0], d[0]
        for j in range(1, STEPS):
            Q = k[j] * Q + d[j]
            A = k[j] * A
        for sh in (1, 2, 4):
            An = jnp.where(sub < sh, one, pltpu.roll(A, sh, 0))
            Qn = jnp.where(sub < sh, 0.0, pltpu.roll(Q, sh, 0))
            Q = Q + A * Qn
            A = A * An
        carry = jnp.where(i == 0, 0.0, r.scarry[s])
        ends = Q + A * carry
        r.scarry[s] = jnp.broadcast_to(ends[7:8], (8, D))
        Q = jnp.where(sub == 0, carry, pltpu.roll(ends, 1, 0))
        for j in range(STEPS):
            at = s * BLK + 8 * j
            place = pl.ds(pl.multiple_of(i * (S * BLK) + at, 8), 8)
            r.to_rate[place, :] = bend[at : at + 8] * (gap[at : at + 8] - Q)
            Q = k[j] * Q + d[j]
            r.state[place, :] = Q


def normalise(values, D):
    mean = jnp.sum(values, axis=1, keepdims=True) * (1.0 / D)
    c = values - mean
    var = jnp.sum(c * c, axis=1, keepdims=True) * (1.0 / D)
    rs = lax.rsqrt(var + 1e-05)
    return c * rs, rs


def norms(i, r, dims):
    S, L, D = dims
    rows = block_rows(i, dims)
    xhat1, rs1 = normalise(r.state[rows, :], D)
    branch = jnp.where(live(i, r, dims), xhat1 * r.g1[...] + r.b1[...], 0.0)
    mid = r.joined[rows, pl.ds(0, D)].astype(F32) + branch
    xhat2, rs2 = normalise(mid, D)
    normed = (xhat2 * r.g2[...] + r.b2[...]).astype(BF16)
    r.xhat1[rows, :] = xhat1
    r.xhat2[rows, :] = xhat2
    r.rs1[rows, :] = rs1
    r.rs2[rows, :] = rs2
    r.mid[rows, :] = mid
    r.normed[rows, :] = normed
    r.normed_t[pl.ds(0, D), rows] = normed.T


def feed_up(i, r, dims):
    S, L, D = dims
    FF = r.wu.shape[1]
    rows = block_rows(i, dims)
    normed, half_t = r.normed[rows, :], r.half_t[:, rows]
    for n in range(FF // FF_STEP):
        cols = slice(n * FF_STEP, (n + 1) * FF_STEP)
        pu = mm(normed, r.wu[:, cols]) + r.bu[:, cols]
        v2 = pu * pu
        s = 1.0 + jnp.tanh(pu * (v2 * (GC * GA) + GC))
        hid = pu * s
        hid16 = hid.astype(BF16)
        r.hidden[rows, cols] = hid16
        r.slope[rows, cols] = s + hid * (2.0 - s) * (v2 * (3.0 * GA * GC) + GC)
        r.dwd_t[:, cols] += mm(half_t, hid16)


def norm_back(dx, xhat, rs, total, by_gain, D):
    ex = dx * xhat
    total[...] += fold(dx)
    by_gain[...] += fold(ex)
    m1 = jnp.sum(dx, axis=1, keepdims=True) * (1.0 / D)
    m2 = jnp.sum(ex, axis=1, keepdims=True) * (1.0 / D)
    return rs * (dx - m1 - xhat * m2)


def feed_down(i, r, dims):
    S, L, D = dims
    FF = r.wu.shape[1]
    rows = block_rows(i, dims)
    half, normed_t = r.half[rows, :], r.normed_t[:, rows]
    for n in range(FF // FF_STEP):
        cols = slice(n * FF_STEP, (n + 1) * FF_STEP)
        gpu = (mm_nt(half, r.wd_rows(n, FF_STEP)) * r.slope[rows, cols]).astype(BF16)
        r.gpu[:, cols] = gpu
        part = mm(normed_t, gpu)
        add_to(r.dwu, cols, part[:D])
        r.gbu[:, cols] += part[D : D + 8]
    gn = mm_nt(r.gpu[...], r.wu[...])
    gmid = r.mixed_cot[rows, :].astype(F32) + norm_back(gn * r.g2[...], r.xhat2[rows, :], r.rs2[rows, :], r.gb2, r.gg2, D)
    r.gmid[rows, :] = gmid
    dx = jnp.where(live(i, r, dims), gmid * r.g1[...], 0.0)
    r.gnorm[rows, :] = norm_back(dx, r.xhat1[rows, :], r.rs1[rows, :], r.gb1, r.gg1, D)


def gates_back(i, r, dims):
    S, L, D = dims
    nb = L // BLK
    rows = block_rows(i, dims)
    sub = sublane((8, D))
    keep = r.keep[rows, :]
    gnorm = r.gnorm[rows, :]
    gs = []
    one = jnp.ones((8, D), F32)
    for s in range(S):
        k = [keep[s * BLK + 8 * j : s * BLK + 8 * j + 8] for j in range(STEPS)]
        g = [gnorm[s * BLK + 8 * j : s * BLK + 8 * j + 8] for j in range(STEPS)]
        A = k[STEPS - 1]
        H = k[STEPS - 1] * g[STEPS - 1]
        for j in range(STEPS - 2, -1, -1):
            H = k[j] * (g[j] + H)
            A = k[j] * A
        for sh in (1, 2, 4):
            An = jnp.where(sub >= 8 - sh, one, pltpu.roll(A, 8 - sh, 0))
            Hn = jnp.where(sub >= 8 - sh, 0.0, pltpu.roll(H, 8 - sh, 0))
            H = H + A * Hn
            A = A * An
        carry = jnp.where(i == nb - 1, 0.0, r.scarry[s])
        ends = H + A * carry
        r.scarry[s] = jnp.broadcast_to(ends[0:1], (8, D))
        H = jnp.where(sub == 7, carry, pltpu.roll(ends, 7, 0))
        out = [None] * STEPS
        for j in range(STEPS - 1, -1, -1):
            out[j] = g[j] + H
            H = k[j] * out[j]
        gs += out
    gs = jnp.concatenate(gs, axis=0)
    gph = jnp.concatenate([gs * r.to_rate[rows, :], gs * r.to_value[rows, :], gs * r.to_fallback[rows, :]], axis=1).astype(BF16)
    gpb = (mm_nt(gph, r.wh[...]) * r.bend[rows, :]).astype(BF16)
    r.gpb[rows, :] = gpb
    part = mm(r.feat_t[:, rows], gph)
    add_to(r.dwh, slice(0, 3 * D), part[:D])
    r.gbh[...] += part[D : D + 8]
    part = mm(r.joined_t[:, rows], gpb)
    add_to(r.dwb, slice(0, D), part[: 2 * D])
    r.gbb[...] += part[2 * D : 2 * D + 8]


def emit(i, r, dims):
    S, L, D = dims
    rows = block_rows(i, dims)
    back = shuffle(True)
    branch = 0.5 * mm(r.hidden[rows, :], flat(r.wd)) + r.bd[...]
    out = (r.mid[rows, :] + jnp.where(live(i, r, dims), branch, 0.0)).astype(BF16)
    for s in range(S):
        r.out[pl.ds(s * L + i * BLK, BLK), :] = mm(back, out[s * BLK : (s + 1) * BLK]).astype(BF16)


def leave(i, r, dims):
    S, L, D = dims
    nb = L // BLK
    rows = block_rows(i, dims)
    sub = sublane((8, D))
    back = shuffle(True)
    gj = mm_nt(r.gpb[rows, :], flat(r.wb))
    gmid = r.gmid[rows, :]
    for s in range(S):
        own = gj[s * BLK : (s + 1) * BLK, :D]
        before = gj[s * BLK : (s + 1) * BLK, D:]
        turned = pltpu.roll(before[:8], 7, 0)
        last = jnp.where(sub == 7, jnp.where(i == nb - 1, 0.0, r.xcarry[s]), turned)
        r.xcarry[s] = turned
        moved = jnp.concatenate([before[8:], last], axis=0)
        grad = (gmid[s * BLK : (s + 1) * BLK] + own + moved).astype(BF16)
        r.ig[pl.ds(s * L + i * BLK, BLK), :] = mm(back, grad).astype(BF16)


SUMS = ("gbb", "gbh", "gg1", "gb1", "gg2", "gb2", "gbu", "gbd")


def set_up(r):
    for name in SUMS + ("dwu", "dwd_t", "dwh", "dwb"):
        ref = getattr(r, name)
        ref[...] = jnp.zeros_like(ref)
    for ref in (r.joined_t, r.feat_t, r.normed_t):
        ref[pl.ds(ref.shape[0] - 16, 16), :] = jnp.ones((16, ref.shape[1]), BF16)


def column_sums(r):
    parts = []
    for name in SUMS:
        if name in ("gbb", "gbh", "gbu"):
            parts.append(getattr(r, name)[0:1, :])
        else:
            part = jnp.sum(getattr(r, name)[...], axis=0, keepdims=True)
            gain = {"gg1": r.g1, "gb1": r.g1, "gg2": r.g2, "gb2": r.g2}.get(name)
            parts.append(part if gain is None else part / gain[...])
    return jnp.concatenate(parts, axis=1)


def sum_widths(D, FF):
    return (D, 3 * D, D, D, D, D, FF, D)


def work_space(S, L, D, FF):
    T = S * L
    v = pltpu.VMEM
    space = dict(
        joined=v((T, 2 * D), BF16), joined_t=v((2 * D + 16, T), BF16), mixed_cot=v((T, D), BF16),
        half=v((T, D), BF16), half_t=v((D, T), BF16), bend=v((T, D), F32),
        feat=v((T, D), BF16), feat_t=v((D + 16, T), BF16), keep=v((T, D), F32),
        to_rate=v((T, D), F32), to_value=v((T, D), F32), to_fallback=v((T, D), F32), state=v((T, D), F32),
        xcarry=v((S, 8, D), F32), scarry=v((S, 8, D), F32), xhat1=v((T, D), F32), xhat2=v((T, D), F32),
        rs1=v((T, 1), F32), rs2=v((T, 1), F32), mid=v((T, D), F32), normed=v((T, D), BF16),
        normed_t=v((D + 16, T), BF16), hidden=v((T, FF), BF16), slope=v((T, FF), F32),
        gpu=v((S * BLK, FF), BF16), dwd_t=v((D, FF), F32),
    )
    for name, width in zip(SUMS, sum_widths(D, FF)):
        space[name] = v((8, width), F32)
    return space


class Refs:
    def wd_rows(self, n, width):
        if len(self.wd.shape) == 2:
            return self.wd[pl.ds(n * width, width), :]
        z, q, c, piece, columns = self.wd.shape
        plane = q * c * piece
        return self.wd[pl.ds(n * width // plane, width // plane)].reshape(width, columns)


def refs_of(names, refs):
    r = Refs()
    for name, ref in zip(names, refs):
        setattr(r, name, ref)
    r.gnorm, r.gmid, r.gpb = r.state, r.xhat2, r.feat
    return r


class Place:
    def __init__(self, n):
        self.n = n
        self.planes = n // (2 * QUAD)
        self.me = lax.axis_index("dp")
        self.c = self.me % 2
        self.q = (self.me // 2) % QUAD
        self.z = self.me // (2 * QUAD)
        self.partner = self.me + 1 - 2 * self.c

    def plane(self, k):
        return (self.z + k) % self.planes

    def corner(self, k):
        return (self.q + k) % QUAD

    def device(self, z, q):
        return (z * QUAD + q) * 2 + self.c

    def peers(self):
        found = [self.device(self.plane(a), self.q) for a in range(1, self.planes)]
        found += [self.device(self.z, self.corner(b)) for b in range(1, QUAD)]
        return found + [self.partner]


class Copies:
    def __init__(self, send, recv):
        self.send, self.recv, self.used, self.open = send, recv, 0, []

    def start(self, src, dst, device):
        k = self.used
        self.used += 1
        copy = pltpu.make_async_remote_copy(
            src_ref=src, dst_ref=dst, send_sem=self.send.at[k], recv_sem=self.recv.at[k],
            device_id=(device,), device_id_type=MESH,
        )
        copy.start()
        self.open.append(copy)
        return copy

    def finish(self):
        for copy in self.open:
            copy.wait_send()


def arrived(copies):
    for copy in copies:
        copy.wait_recv()


def cut(values):
    half = values.shape[-1] // 2
    return jnp.concatenate([values[..., :half], values[..., half:]], axis=-2)


def uncut(values):
    return jnp.concatenate([values[..., :8, :], values[..., 8:, :]], axis=-1)


def same(values):
    return values


class Share:
    def __init__(self, r, name, cutter, copies, place, plane_first):
        self.r, self.name, self.cut, self.copies, self.p = r, name, cutter, copies, place
        self.plane_first = plane_first

    def ref(self, kind):
        return getattr(self.r, kind + self.name)

    def mine(self, ref):
        return ref[self.p.z] if self.plane_first else ref[:, self.p.q]

    def send(self, ref, target, along_planes):
        p, sent = self.p, []
        for k in range(1, p.planes if along_planes else QUAD):
            if along_planes:
                part, device = p.plane(k), p.device(p.plane(k), p.q)
            else:
                part, device = p.corner(k), p.device(p.z, p.corner(k))
            source = ref.at[:, part] if len(ref.shape) == 4 and not along_planes else ref.at[part]
            sent.append(self.copies.start(source, target.at[k - 1], device))
        return sent

    def pair(self):
        p = self.p
        self.ref("cs")[...] = self.cut(self.ref("dw")[:, :, 1 - p.c]).astype(BF16)
        self.sent = [self.copies.start(self.ref("cs"), self.ref("cr"), p.partner)]

    def spread(self):
        arrived(self.sent)
        total = self.cut(self.ref("dw")[:, :, self.p.c]) + self.ref("cr")[...].astype(F32)
        self.ref("xs")[...] = total.astype(BF16)
        self.sent = self.send(self.ref("xs"), self.ref("xr"), self.plane_first)

    def climb(self):
        p = self.p
        arrived(self.sent)
        own = self.ref("dw")[p.z, :, p.c] if self.plane_first else self.ref("dw")[:, p.q, p.c]
        total = self.cut(own) + self.mine(self.ref("cr")).astype(F32)
        for k in range(len(self.sent)):
            total = total + self.ref("xr")[k].astype(F32)
        self.ref("ac")[...] = total
        self.ref("zs")[...] = total.astype(BF16)
        self.sent = self.send(self.ref("zs"), self.ref("zr"), not self.plane_first)

    def land(self):
        arrived(self.sent)
        total = self.ref("ac")[self.p.q if self.plane_first else self.p.z]
        for k in range(len(self.sent)):
            total = total + self.ref("zr")[k].astype(F32)
        return total


def share_space(name, n, rows, columns, cutting, plane_first):
    Z, v = n // (2 * QUAD), pltpu.VMEM
    R, C = (2 * rows, columns // 2) if cutting else (rows, columns)
    first, second = (Z, QUAD) if plane_first else (QUAD, Z)
    return {
        "dw" + name: v((Z, QUAD, 2, rows, columns), F32),
        "cs" + name: v((Z, QUAD, R, C), BF16),
        "cr" + name: v((Z, QUAD, R, C), BF16),
        "xs" + name: v((Z, QUAD, R, C), BF16),
        "xr" + name: v((first - 1, second, R, C), BF16),
        "ac" + name: v((second, R, C), F32),
        "zs" + name: v((second, R, C), BF16),
        "zr" + name: v((second - 1, R, C), BF16),
    }


def segments(n, D, FF):
    found, lane, offset = [], 0, 0
    for name, width in zip(("bb", "bh", "g1", "b1", "g2", "b2", "bu", "bd"), sum_widths(D, FF)):
        found.append((name, lane, width, width // n, offset))
        lane, offset = lane + width, offset + width // n
    return found


def fill_pick(r, n, D, FF):
    for name, lane, width, own, offset in segments(n, D, FF):
        l = lax.broadcasted_iota(jnp.int32, (width, 128), 0).astype(F32)
        k = lax.broadcasted_iota(jnp.int32, (width, 128), 1).astype(F32)
        place = l - own * jnp.floor((l + 0.5) * (1.0 / own)) + offset
        r.pick[pl.ds(lane, width), :] = jnp.where(place == k, 1.0, 0.0).astype(BF16)


def owners(n, D, FF):
    parts, Z = [], n // (2 * QUAD)
    for name, lane, width, own, offset in segments(n, D, FF):
        l = lax.broadcasted_iota(jnp.int32, (n, width), 1).astype(F32)
        row = lax.broadcasted_iota(jnp.int32, (n, width), 0)
        z, q, c = row % Z, row // Z % QUAD, row // (Z * QUAD)
        device = ((z * QUAD + q) * 2 + c).astype(F32)
        parts.append(jnp.floor((l + 0.5) * (1.0 / own)) == device)
    return jnp.concatenate(parts, axis=1)


ROWS = ("gback", "gheads", "gup", "gdown", "gvec")
OWN = tuple("own_" + name for name in ("bb", "bh", "g1", "b1", "g2", "b2", "bu", "bd"))
INPUTS = ("lengths", "x_hbm", "cot_hbm", "wb_own", "wh_own", "wu_own", "wd_own") + OWN
OUTPUTS = ("out", "ig") + ROWS


def mega(names, dims, n, FF, *refs):
    r = refs_of(names, refs)
    r.x, r.cot = r.out, r.ig
    S, L, D = dims
    nb = L // BLK
    p = Place(n)
    copies = Copies(r.send, r.recv)

    def run(f, first, last, down=False):
        def step(i, c):
            f(nb - 1 - i if down else i, r, dims)
            return c
        lax.fori_loop(first, last, step, 0, unroll=True)

    barrier = pltpu.get_barrier_semaphore()
    for peer in p.peers():
        pl.semaphore_signal(barrier, inc=1, device_id=(peer,), device_id_type=MESH)

    loads = [
        pltpu.make_async_copy(src, dst, r.local.at[k])
        for k, (src, dst) in enumerate((
            (r.wb_own, r.wb.at[p.z, p.q, p.c]),
            (r.wh_own, r.wh_mine), (r.wu_own, r.wu_mine), (r.wd_own, r.wd.at[p.z, p.q, p.c]),
            *((getattr(r, name), getattr(r, "my_" + name)) for name in OWN),
            (r.x_hbm, r.x), (r.cot_hbm, r.cot),
        ))
    ]
    for load in loads:
        load.start()
    r.vec_rows[...] = jnp.zeros_like(r.vec_rows)
    for load in loads[:-2]:
        load.wait()
    own_row = jnp.zeros((1, 128), F32)
    for k, (name, lane, width, own, offset) in enumerate(segments(n, D, FF)):
        r.vec_rows[pl.ds(k, 1), pl.ds(0, own)] = getattr(r, "my_" + OWN[k])[...].astype(F32)
        own_row = own_row + pltpu.roll(r.vec_rows[pl.ds(k, 1), :], offset, 1)
    r.vec[p.c, p.q, pl.ds(p.z, 1)] = own_row
    r.wh_cut[p.z, p.q, p.c] = cut(r.wh_mine[...].astype(F32)).astype(BF16)
    r.wu_cut[p.z, p.q, p.c] = cut(r.wu_mine[...].astype(F32)).astype(BF16)
    pl.semaphore_wait(barrier, len(p.peers()))

    def to_planes(own):
        return [copies.start(own, own, p.device(p.plane(a), p.q)) for a in range(1, p.planes)]

    def to_corners(own):
        return [copies.start(own, own, p.device(p.z, p.corner(b))) for b in range(1, QUAD)]

    def to_partner(own):
        return [copies.start(own, own, p.partner)]

    weights = (r.wb, r.wh_cut, r.wu_cut, r.wd)
    wb_in = to_planes(r.wb.at[p.z, p.q, p.c])
    vec_in = to_planes(r.vec.at[p.c, p.q, pl.ds(p.z, 1)])
    wh_in, up_in, down_in = (to_planes(ref.at[p.z, p.q, p.c]) for ref in weights[1:])

    set_up(r)
    arrived(wb_in)
    wb_in = to_corners(r.wb.at[:, p.q, p.c])
    arrived(vec_in)
    vec_in = to_corners(r.vec.at[p.c, p.q])
    arrived(wh_in)
    wh_in = to_corners(r.wh_cut.at[:, p.q, p.c])
    for load in loads[-2:]:
        load.wait()
    run(enter, 0, nb)
    fill_pick(r, n, D, FF)
    arrived(wb_in)
    wb_in = to_partner(r.wb.at[:, :, p.c])
    arrived(vec_in)
    vec_in = to_partner(r.vec.at[p.c])
    arrived(up_in)
    up_in = to_corners(r.wu_cut.at[:, p.q, p.c])
    arrived(down_in)
    down_in = to_corners(r.wd.at[:, p.q, p.c])
    arrived(wb_in)
    arrived(vec_in)
    spread = mm_nt(r.vec[...].reshape(n, 128).astype(BF16), r.pick[...])
    vectors = jnp.sum(jnp.where(owners(n, D, FF), spread, 0.0), axis=0, keepdims=True)
    for name, lane, width, own, offset in segments(n, D, FF):
        getattr(r, name)[...] = vectors[:, lane : lane + width]

    arrived(wh_in)
    wh_in = to_partner(r.wh_cut.at[:, :, p.c])
    run(backbone, 0, nb)
    arrived(wh_in)
    r.wh[...] = uncut(r.wh_cut[...].astype(F32)).reshape(D, 3 * D).astype(BF16)
    run(gates, 0, nb)
    arrived(up_in)
    up_in = to_partner(r.wu_cut.at[:, :, p.c])
    run(norms, 0, nb)
    arrived(up_in)
    r.wu[...] = uncut(r.wu_cut[...].astype(F32)).reshape(D, FF).astype(BF16)
    run(feed_up, 0, 1)
    arrived(down_in)
    down_in = to_partner(r.wd.at[:, :, p.c])
    run(feed_up, 1, nb)
    arrived(down_in)

    up = Share(r, "u", cut, copies, p, UP_PLANE)
    down = Share(r, "d", same, copies, p, DOWN_PLANE)
    heads = Share(r, "h", cut, copies, p, HEADS_PLANE)
    back = Share(r, "b", same, copies, p, BACK_PLANE)
    r.dwd[...] = r.dwd_t[...].T.reshape(r.dwd.shape)
    down.pair()
    run(feed_down, 0, 2)
    down.spread()
    run(feed_down, 2, nb)
    up.pair()
    run(gates_back, 0, 2, True)
    up.spread()
    run(gates_back, 2, nb, True)
    heads.pair()
    back.pair()

    rest, rows = jnp.where(owners(n, D, FF), column_sums(r), 0.0), None
    for _ in range(3):
        part = rest.astype(BF16)
        rest = rest - part.astype(F32)
        row = mm(part, r.pick[...])
        rows = row if rows is None else rows + row
    r.vs[...] = rows.reshape(r.vs.shape)
    vec_out = [copies.start(r.vs.at[1 - p.c], r.vr, p.partner)]
    heads.spread()
    back.spread()
    arrived(vec_out)
    r.va[...] = r.vs[p.c] + r.vr[...]
    vec_out = []
    for b in range(1, QUAD):
        q = p.corner(b)
        vec_out.append(copies.start(r.va.at[q], r.vx.at[b - 1], p.device(p.z, q)))
    down.climb()
    up.climb()
    run(leave, 0, nb, True)
    heads.climb()
    back.climb()
    arrived(vec_out)
    total = r.va[p.q]
    for b in range(QUAD - 1):
        total = total + r.vx[b]
    r.vz[...] = total
    vec_out = []
    for a in range(1, p.planes):
        z = p.plane(a)
        vec_out.append(copies.start(r.vz.at[pl.ds(z, 1)], r.vt.at[pl.ds(a - 1, 1)], p.device(z, p.q)))
    run(emit, 0, nb)
    r.gup[...] = uncut(up.land())
    r.gdown[...] = down.land()
    r.gheads[...] = uncut(heads.land())
    r.gback[...] = back.land()
    arrived(vec_out)
    r.gvec[...] = r.vz[pl.ds(p.z, 1), :] + jnp.sum(r.vt[...], axis=0, keepdims=True)
    copies.finish()


def quick(lengths, x, cot, wb, wh, wu, wd, vectors, n):
    vectors = [v.reshape(1, -1) for v in vectors]
    S = lengths.shape[0]
    T, D = x.shape
    L, FF = T // S, wu.shape[1]
    Z, v = n // (2 * QUAD), pltpu.VMEM
    space = work_space(S, L, D, FF)
    rb, rh, ru, rd = wb.shape[0], wh.shape[0], wu.shape[0], wd.shape[0]
    space.update(
        wb=v((Z, QUAD, 2, rb, D), BF16), wd=v((Z, QUAD, 2, rd, D), BF16),
        wh_cut=v((Z, QUAD, 2, 2 * rh, 3 * D // 2), BF16), wu_cut=v((Z, QUAD, 2, 2 * ru, FF // 2), BF16),
        wh=v((D, 3 * D), BF16), wu=v((D, FF), BF16), wh_mine=v((rh, 3 * D), BF16), wu_mine=v((ru, FF), BF16),
        vec=v((2, QUAD, Z, 128), F32), pick=v((sum(sum_widths(D, FF)), 128), BF16),
        vs=v((2, QUAD, Z, 128), F32), vr=v((QUAD, Z, 128), F32), va=v((QUAD, Z, 128), F32),
        vx=v((QUAD - 1, Z, 128), F32), vz=v((Z, 128), F32), vt=v((Z - 1, 128), F32),
        local=pltpu.SemaphoreType.DMA((14,)), send=pltpu.SemaphoreType.DMA((72,)), recv=pltpu.SemaphoreType.DMA((72,)),
    )
    for name, lane, width, own, offset in segments(n, D, FF):
        space[name] = v((1, width), F32)
        space["my_own_" + name] = v((1, own), BF16)
    space["vec_rows"] = v((8, 128), F32)
    space.update(share_space("u", n, ru, FF, True, UP_PLANE))
    space.update(share_space("d", n, rd, D, False, DOWN_PLANE))
    space.update(share_space("h", n, rh, 3 * D, True, HEADS_PLANE))
    space.update(share_space("b", n, rb, D, False, BACK_PLANE))
    shapes = (
        v((T, D), BF16), v((T, D), BF16),
        v((rb, D), F32), v((rh, 3 * D), F32), v((ru, FF), F32), v((rd, D), F32), v((1, 128), F32),
    )
    hbm, vmem = pl.BlockSpec(memory_space=pl.ANY), pl.BlockSpec(memory_space=pltpu.VMEM)
    results = pl.pallas_call(
        functools.partial(mega, INPUTS + OUTPUTS + tuple(space), (S, L, D), n, FF),
        out_shape=shapes,
        in_specs=[pl.BlockSpec(memory_space=pltpu.SMEM)] + [hbm] * 14,
        out_specs=[vmem] * 7,
        scratch_shapes=list(space.values()),
        compiler_params=pltpu.CompilerParams(collective_id=0, has_side_effects=True, vmem_limit_bytes=60 << 20),
    )(lengths, x, cot, wb, wh, wu, wd, *vectors)
    return hand_over(results, [own for name, lane, width, own, offset in segments(n, D, FF)])


def hand_over_kernel(widths, *refs):
    count = 6
    sources, vec, targets = refs[:count], refs[count], refs[count + 1 : 2 * count + 1]
    smalls, sem = refs[2 * count + 1 : -1], refs[-1]
    moves = [pltpu.make_async_copy(s, t, sem.at[k]) for k, (s, t) in enumerate(zip(sources, targets))]
    for move in moves:
        move.start()
    at = 0
    for small, width in zip(smalls, widths):
        small[...] = pltpu.roll(vec[...], (128 - at) % 128, 1)[:, :width]
        at += width
    for move in moves:
        move.wait()


def hand_over(results, widths):
    hbm, vmem = pl.BlockSpec(memory_space=pl.ANY), pl.BlockSpec(memory_space=pltpu.VMEM)
    shapes = [jax.ShapeDtypeStruct(a.shape, a.dtype) for a in results[:6]]
    shapes += [jax.ShapeDtypeStruct((1, w), F32) for w in widths]
    return pl.pallas_call(
        functools.partial(hand_over_kernel, widths),
        out_shape=shapes,
        in_specs=[vmem] * 7,
        out_specs=[hbm] * 6 + [vmem] * len(widths),
        scratch_shapes=[pltpu.SemaphoreType.DMA((6,))],
        compiler_params=pltpu.CompilerParams(vmem_limit_bytes=16 << 20),
    )(*results)


def plain(names, dims, *refs):
    r = refs_of(names, refs)
    S, L, D = dims
    nb = L // BLK

    def run(f, down=False):
        def step(i, c):
            f(nb - 1 - i if down else i, r, dims)
            return c
        lax.fori_loop(0, nb, step, 0)

    set_up(r)
    for f in (enter, backbone, gates, norms, feed_up, feed_down, emit):
        run(f)
    run(gates_back, True)
    run(leave, True)
    r.gdown[...] = r.dwd_t[...].T
    sums, at = column_sums(r), 0
    for name in SUMS:
        ref = getattr(r, "all" + name)
        ref[...] = sums[:, at : at + ref.shape[1]]
        at += ref.shape[1]


def whole(lengths, x, cot, matrices, vectors):
    S = lengths.shape[0]
    T, D = x.shape
    L, FF = T // S, matrices[2].shape[1]
    space = work_space(S, L, D, FF)
    names = ("lengths", "x", "cot", "wb", "wh", "wu", "wd", "bb", "bh", "g1", "b1", "g2", "b2", "bu", "bd")
    names += ("out", "ig", "dwb", "dwh", "dwu", "gdown") + tuple("all" + name for name in SUMS) + tuple(space)
    row = lambda a, b: jax.ShapeDtypeStruct((a, b), F32)
    shapes = (jax.ShapeDtypeStruct((T, D), BF16),) * 2
    shapes += tuple(row(*m.shape) for m in matrices) + tuple(row(1, width) for width in sum_widths(D, FF))
    vmem = pl.BlockSpec(memory_space=pltpu.VMEM)
    return pl.pallas_call(
        functools.partial(plain, names, (S, L, D)),
        out_shape=shapes,
        in_specs=[pl.BlockSpec(memory_space=pltpu.SMEM)] + [vmem] * 14,
        out_specs=[vmem] * len(shapes),
        scratch_shapes=list(space.values()),
        compiler_params=pltpu.CompilerParams(vmem_limit_bytes=62 << 20),
    )(lengths, x, cot, *matrices, *(v.astype(F32).reshape(1, -1) for v in vectors))


def by_collectives(lengths, x, cot, matrices, vectors):
    gather = lambda a: lax.all_gather(a, "dp", axis=0, tiled=True)
    scatter = lambda a: lax.psum_scatter(a, "dp", scatter_dimension=0, tiled=True)
    results = whole(lengths, x, cot, [gather(m) for m in matrices], [gather(v) for v in vectors])
    return results[:2], [scatter(m) for m in results[2:6]], [scatter(v[0]) for v in results[6:]]


def by_kernel(lengths, x, cot, matrices, vectors, n):
    results = quick(lengths, x, cot, *matrices, vectors, n)
    return results[:2], results[2:6], [row[0] for row in results[6:]]


def in_tiles(n, back_w, heads_w, up_w, down_w):
    rows = 2 * QUAD * down_w.shape[0]
    return (
        n % (2 * QUAD) == 0 and heads_w.shape[0] == 8 and up_w.shape[0] == 8
        and back_w.shape[0] % 16 == 0 and down_w.shape[0] % 16 == 0 and FF_STEP % rows == 0
    )


def local(n, block_in, lengths, back_w, back_b, heads_w, heads_b, norm1_gain, norm1_bias, norm2_gain, norm2_bias,
          up_w, up_b, down_w, down_b, cotangent):
    matrices = (back_w, heads_w, up_w, down_w)
    vectors = (back_b, heads_b, norm1_gain, norm1_bias, norm2_gain, norm2_bias, up_b, down_b)
    if in_tiles(n, *matrices):
        big, weights, small = by_kernel(lengths, block_in, cotangent, matrices, vectors, n)
    else:
        big, weights, small = by_collectives(lengths, block_in, cotangent, matrices, vectors)
    gback, gheads, gup, gdown = weights
    gb, gh, gg1, gb1, gg2, gb2, gu, gd = small
    return *big, gback, gb, gheads, gh, gg1, gb1, gg2, gb2, gup, gu, gdown, gd


def solution(mesh):
    n = mesh.shape["dp"]
    m, v = P("dp", None), P("dp")
    return jax.shard_map(
        functools.partial(local, n), mesh=mesh,
        in_specs=(m, v, m, v, m, v, v, v, v, v, m, v, m, v, m),
        out_specs=(m, m, m, v, m, v, v, v, v, v, m, v, m, v), check_vma=False,
    )
```

```python
import functools
import jax
import jax.numpy as jnp
from jax import lax
from jax.experimental import pallas as pl
from jax.experimental.pallas import tpu as pltpu
from jax.sharding import PartitionSpec as P

BLK = 256
LANES = 8
STEPS = BLK // LANES
QUAD = 4
FF_STEP = 256
UP_PLANE, DOWN_PLANE, HEADS_PLANE, BACK_PLANE = False, False, False, True
F32 = jnp.float32
BF16 = jnp.bfloat16
MESH = pl.DeviceIdType.MESH
GC = 0.7978845608028654
GA = 0.044715


def mm(a, b):
    return lax.dot_general(a, b, (((1,), (0,)), ((), ())), preferred_element_type=F32)


def mm_nt(a, b):
    return lax.dot_general(a, b, (((1,), (1,)), ((), ())), preferred_element_type=F32)


def mm_tn(a, b):
    return lax.dot_general(a, b, (((0,), (0,)), ((), ())), preferred_element_type=F32)


def shuffle(transposed=False):
    row = lax.broadcasted_iota(jnp.int32, (BLK, BLK), 0)
    col = lax.broadcasted_iota(jnp.int32, (BLK, BLK), 1)
    if transposed:
        row, col = col, row
    return jnp.where((row & 7) * STEPS + (row >> 3) == col, 1.0, 0.0).astype(BF16)


def fold(values):
    return jnp.sum(values.reshape(values.shape[0] // 8, 8, values.shape[1]), axis=0)


def sublane(shape):
    return lax.broadcasted_iota(jnp.int32, shape, 0)


def flat(ref):
    values = ref[...]
    return values.reshape(-1, values.shape[-1])


def block_rows(i, dims):
    return pl.ds(pl.multiple_of(i * (dims[0] * BLK), dims[0] * BLK), dims[0] * BLK)


def add_to(ref, columns, values):
    ref[..., columns] += values.reshape(ref.shape[:-1] + values.shape[-1:])


def live(i, r, dims):
    S, L, D = dims
    row = lax.broadcasted_iota(jnp.int32, (BLK, D), 0)
    time = (row & 7) * STEPS + (row >> 3) + i * BLK
    return jnp.concatenate([time < r.lengths[s] for s in range(S)], axis=0)


def enter(i, r, dims):
    S, L, D = dims
    order = shuffle()
    sub = sublane((8, D))
    joined, cots = [], []
    for s in range(S):
        cots.append(mm(order, r.cot[pl.ds(s * L + i * BLK, BLK), :]))
        mixed = mm(order, r.x[pl.ds(s * L + i * BLK, BLK), :])
        turned = pltpu.roll(mixed[BLK - 8 :], 1, 0)
        first = jnp.where(sub == 0, jnp.where(i == 0, 0.0, r.xcarry[s]), turned)
        r.xcarry[s] = turned
        before = jnp.concatenate([first, mixed[: BLK - 8]], axis=0)
        joined.append(jnp.concatenate([mixed, before], axis=1))
    rows = block_rows(i, dims)
    joined = jnp.concatenate(joined, axis=0).astype(BF16)
    r.joined[rows, :] = joined
    r.joined_t[pl.ds(0, 2 * D), rows] = joined.T
    cot = jnp.concatenate(cots, axis=0)
    r.mixed_cot[rows, :] = cot.astype(BF16)
    gout = jnp.where(live(i, r, dims), cot, 0.0)
    r.gbd[...] += fold(gout)
    half = (0.5 * gout).astype(BF16)
    r.half[rows, :] = half
    r.half_t[:, rows] = half.T


def backbone(i, r, dims):
    S, L, D = dims
    rows = block_rows(i, dims)
    inner = jnp.tanh(0.666 * (mm(r.joined[rows, :], flat(r.wb)) + r.bb[...]))
    r.bend[rows, :] = (1.7159 * 0.666) * (1.0 - inner * inner)
    feat = (1.7159 * inner).astype(BF16)
    r.feat[rows, :] = feat
    r.feat_t[pl.ds(0, D), rows] = feat.T


def gates(i, r, dims):
    S, L, D = dims
    rows = block_rows(i, dims)
    sub = sublane((8, D))
    heads = mm(r.feat[rows, :], r.wh[...]) + r.bh[...]
    o = 0.5 * jnp.tanh(0.5 * heads[:, :D]) + 0.5
    v = jnp.tanh(heads[:, D : 2 * D])
    f = jnp.tanh(heads[:, 2 * D :])
    keep = 1.0 - o
    gap = v - f
    drive = f + o * gap
    r.keep[rows, :] = keep
    r.to_value[rows, :] = o * (1.0 - v * v)
    r.to_fallback[rows, :] = keep * (1.0 - f * f)
    bend = o * keep
    one = jnp.ones((8, D), F32)
    for s in range(S):
        k = [keep[s * BLK + 8 * j : s * BLK + 8 * j + 8] for j in range(STEPS)]
        d = [drive[s * BLK + 8 * j : s * BLK + 8 * j + 8] for j in range(STEPS)]
        A, Q = k[0], d[0]
        for j in range(1, STEPS):
            Q = k[j] * Q + d[j]
            A = k[j] * A
        for sh in (1, 2, 4):
            An = jnp.where(sub < sh, one, pltpu.roll(A, sh, 0))
            Qn = jnp.where(sub < sh, 0.0, pltpu.roll(Q, sh, 0))
            Q = Q + A * Qn
            A = A * An
        carry = jnp.where(i == 0, 0.0, r.scarry[s])
        ends = Q + A * carry
        r.scarry[s] = jnp.broadcast_to(ends[7:8], (8, D))
        Q = jnp.where(sub == 0, carry, pltpu.roll(ends, 1, 0))
        for j in range(STEPS):
            at = s * BLK + 8 * j
            place = pl.ds(pl.multiple_of(i * (S * BLK) + at, 8), 8)
            r.to_rate[place, :] = bend[at : at + 8] * (gap[at : at + 8] - Q)
            Q = k[j] * Q + d[j]
            r.state[place, :] = Q


def normalise(values, D):
    mean = jnp.sum(values, axis=1, keepdims=True) * (1.0 / D)
    c = values - mean
    var = jnp.sum(c * c, axis=1, keepdims=True) * (1.0 / D)
    rs = lax.rsqrt(var + 1e-05)
    return c * rs, rs


def norms(i, r, dims):
    S, L, D = dims
    rows = block_rows(i, dims)
    xhat1, rs1 = normalise(r.state[rows, :], D)
    branch = jnp.where(live(i, r, dims), xhat1 * r.g1[...] + r.b1[...], 0.0)
    mid = r.joined[rows, pl.ds(0, D)].astype(F32) + branch
    xhat2, rs2 = normalise(mid, D)
    normed = (xhat2 * r.g2[...] + r.b2[...]).astype(BF16)
    r.xhat1[rows, :] = xhat1
    r.xhat2[rows, :] = xhat2
    r.rs1[rows, :] = rs1
    r.rs2[rows, :] = rs2
    r.mid[rows, :] = mid
    r.normed[rows, :] = normed
    r.normed_t[pl.ds(0, D), rows] = normed.T


def feed_up(i, n, r, dims):
    rows, cols = block_rows(i, dims), slice(n * FF_STEP, (n + 1) * FF_STEP)
    pu = mm(r.normed[rows, :], r.wu[:, cols]) + r.bu[:, cols]
    v2 = pu * pu
    s = 1.0 + jnp.tanh(pu * (v2 * (GC * GA) + GC))
    hid = pu * s
    hid16 = hid.astype(BF16)
    r.hidden[rows, cols] = hid16
    r.slope[i % 2, :, cols] = s + hid * (2.0 - s) * (v2 * (3.0 * GA * GC) + GC)
    r.dwd_t[:, cols] += mm(r.half_t[:, rows], hid16)


def feed_down(i, n, r, dims):
    D = dims[2]
    rows, cols = block_rows(i, dims), slice(n * FF_STEP, (n + 1) * FF_STEP)
    gpu = (mm_nt(r.half[rows, :], r.wd_rows(n, FF_STEP)) * r.slope[i % 2, :, cols]).astype(BF16)
    r.gpu[i % 2, :, cols] = gpu
    part = mm(r.normed_t[:, rows], gpu)
    add_to(r.dwu, cols, part[:D])
    r.gbu[:, cols] += part[D : D + 8]


def norm_back(dx, xhat, rs, total, by_gain, D):
    ex = dx * xhat
    total[...] += fold(dx)
    by_gain[...] += fold(ex)
    m1 = jnp.sum(dx, axis=1, keepdims=True) * (1.0 / D)
    m2 = jnp.sum(ex, axis=1, keepdims=True) * (1.0 / D)
    return rs * (dx - m1 - xhat * m2)


def norms_back(i, r, dims):
    S, L, D = dims
    rows = block_rows(i, dims)
    gn = mm_nt(r.gpu[i % 2], r.wu[...])
    gmid = r.mixed_cot[rows, :].astype(F32) + norm_back(gn * r.g2[...], r.xhat2[rows, :], r.rs2[rows, :], r.gb2, r.gg2, D)
    r.gmid[rows, :] = gmid
    dx = jnp.where(live(i, r, dims), gmid * r.g1[...], 0.0)
    r.gnorm[rows, :] = norm_back(dx, r.xhat1[rows, :], r.rs1[rows, :], r.gb1, r.gg1, D)


def gates_back(i, r, dims):
    S, L, D = dims
    nb = L // BLK
    rows = block_rows(i, dims)
    sub = sublane((8, D))
    keep = r.keep[rows, :]
    gnorm = r.gnorm[rows, :]
    gs = []
    one = jnp.ones((8, D), F32)
    for s in range(S):
        k = [keep[s * BLK + 8 * j : s * BLK + 8 * j + 8] for j in range(STEPS)]
        g = [gnorm[s * BLK + 8 * j : s * BLK + 8 * j + 8] for j in range(STEPS)]
        A = k[STEPS - 1]
        H = k[STEPS - 1] * g[STEPS - 1]
        for j in range(STEPS - 2, -1, -1):
            H = k[j] * (g[j] + H)
            A = k[j] * A
        for sh in (1, 2, 4):
            An = jnp.where(sub >= 8 - sh, one, pltpu.roll(A, 8 - sh, 0))
            Hn = jnp.where(sub >= 8 - sh, 0.0, pltpu.roll(H, 8 - sh, 0))
            H = H + A * Hn
            A = A * An
        carry = jnp.where(i == nb - 1, 0.0, r.scarry[s])
        ends = H + A * carry
        r.scarry[s] = jnp.broadcast_to(ends[0:1], (8, D))
        H = jnp.where(sub == 7, carry, pltpu.roll(ends, 7, 0))
        out = [None] * STEPS
        for j in range(STEPS - 1, -1, -1):
            out[j] = g[j] + H
            H = k[j] * out[j]
        gs += out
    gs = jnp.concatenate(gs, axis=0)
    gph = jnp.concatenate([gs * r.to_rate[rows, :], gs * r.to_value[rows, :], gs * r.to_fallback[rows, :]], axis=1).astype(BF16)
    gpb = (mm_nt(gph, r.wh[...]) * r.bend[rows, :]).astype(BF16)
    r.gpb[rows, :] = gpb
    part = mm(r.feat_t[:, rows], gph)
    add_to(r.dwh, slice(0, 3 * D), part[:D])
    r.gbh[...] += part[D : D + 8]
    part = mm(r.joined_t[:, rows], gpb)
    add_to(r.dwb, slice(0, D), part[: 2 * D])
    r.gbb[...] += part[2 * D : 2 * D + 8]


def middle(r, dims, after):
    nb = dims[1] // BLK
    for step in range(nb + 1):
        for n in range(r.wu.shape[1] // FF_STEP):
            if step < nb:
                feed_up(nb - 1 - step, n, r, dims)
            if 0 <= step - 1 < nb:
                feed_down(nb - 1 - (step - 1), n, r, dims)
        if step:
            norms_back(nb - step, r, dims)
        for action in after.get(step, ()):
            action()
    for i in reversed(range(nb)):
        gates_back(i, r, dims)
        if i == nb // 2:
            for action in after.get(nb + 1, ()):
                action()


def emit(i, r, dims):
    S, L, D = dims
    rows = block_rows(i, dims)
    back = shuffle(True)
    branch = 0.5 * mm(r.hidden[rows, :], flat(r.wd)) + r.bd[...]
    out = (r.mid[rows, :] + jnp.where(live(i, r, dims), branch, 0.0)).astype(BF16)
    for s in range(S):
        r.out[pl.ds(s * L + i * BLK, BLK), :] = mm(back, out[s * BLK : (s + 1) * BLK]).astype(BF16)


def leave(i, r, dims):
    S, L, D = dims
    nb = L // BLK
    rows = block_rows(i, dims)
    sub = sublane((8, D))
    back = shuffle(True)
    gj = mm_nt(r.gpb[rows, :], flat(r.wb))
    gmid = r.gmid[rows, :]
    for s in range(S):
        own = gj[s * BLK : (s + 1) * BLK, :D]
        before = gj[s * BLK : (s + 1) * BLK, D:]
        turned = pltpu.roll(before[:8], 7, 0)
        last = jnp.where(sub == 7, jnp.where(i == nb - 1, 0.0, r.xcarry[s]), turned)
        r.xcarry[s] = turned
        moved = jnp.concatenate([before[8:], last], axis=0)
        grad = (gmid[s * BLK : (s + 1) * BLK] + own + moved).astype(BF16)
        r.ig[pl.ds(s * L + i * BLK, BLK), :] = mm(back, grad).astype(BF16)


SUMS = ("gbb", "gbh", "gg1", "gb1", "gg2", "gb2", "gbu", "gbd")


def set_up(r):
    for name in SUMS + ("dwu", "dwd_t", "dwh", "dwb"):
        ref = getattr(r, name)
        ref[...] = jnp.zeros_like(ref)
    for ref in (r.joined_t, r.feat_t, r.normed_t):
        ref[pl.ds(ref.shape[0] - 16, 16), :] = jnp.ones((16, ref.shape[1]), BF16)


def column_sums(r):
    parts = []
    for name in SUMS:
        if name in ("gbb", "gbh", "gbu"):
            parts.append(getattr(r, name)[0:1, :])
        else:
            part = jnp.sum(getattr(r, name)[...], axis=0, keepdims=True)
            gain = {"gg1": r.g1, "gb1": r.g1, "gg2": r.g2, "gb2": r.g2}.get(name)
            parts.append(part if gain is None else part / gain[...])
    return jnp.concatenate(parts, axis=1)


def sum_widths(D, FF):
    return (D, 3 * D, D, D, D, D, FF, D)


def work_space(S, L, D, FF):
    T = S * L
    v = pltpu.VMEM
    space = dict(
        joined=v((T, 2 * D), BF16), joined_t=v((2 * D + 16, T), BF16), mixed_cot=v((T, D), BF16),
        half=v((T, D), BF16), half_t=v((D, T), BF16), bend=v((T, D), F32),
        feat=v((T, D), BF16), feat_t=v((D + 16, T), BF16), keep=v((T, D), F32),
        to_rate=v((T, D), F32), to_value=v((T, D), F32), to_fallback=v((T, D), F32), state=v((T, D), F32),
        xcarry=v((S, 8, D), F32), scarry=v((S, 8, D), F32), xhat1=v((T, D), F32), xhat2=v((T, D), F32),
        rs1=v((T, 1), F32), rs2=v((T, 1), F32), mid=v((T, D), F32), normed=v((T, D), BF16),
        normed_t=v((D + 16, T), BF16), hidden=v((T, FF), BF16), slope=v((2, S * BLK, FF), F32),
        gpu=v((2, S * BLK, FF), BF16), dwd_t=v((D, FF), F32),
    )
    for name, width in zip(SUMS, sum_widths(D, FF)):
        space[name] = v((8, width), F32)
    return space


class Refs:
    def wd_rows(self, n, width):
        if len(self.wd.shape) == 2:
            return self.wd[pl.ds(n * width, width), :]
        z, q, c, piece, columns = self.wd.shape
        plane = q * c * piece
        return self.wd[pl.ds(n * width // plane, width // plane)].reshape(width, columns)


def refs_of(names, refs):
    r = Refs()
    for name, ref in zip(names, refs):
        setattr(r, name, ref)
    r.gnorm, r.gmid, r.gpb = r.state, r.xhat2, r.feat
    return r


class Place:
    def __init__(self, n):
        self.n = n
        self.planes = n // (2 * QUAD)
        self.me = lax.axis_index("dp")
        self.c = self.me % 2
        self.q = (self.me // 2) % QUAD
        self.z = self.me // (2 * QUAD)
        self.partner = self.me + 1 - 2 * self.c

    def plane(self, k):
        return (self.z + k) % self.planes

    def corner(self, k):
        return (self.q + k) % QUAD

    def device(self, z, q):
        return (z * QUAD + q) * 2 + self.c

    def peers(self):
        found = [self.device(self.plane(a), self.q) for a in range(1, self.planes)]
        found += [self.device(self.z, self.corner(b)) for b in range(1, QUAD)]
        return found + [self.partner]


class Copies:
    def __init__(self, send, recv):
        self.send, self.recv, self.groups = send, recv, 0
        self.open = []

    def group(self, whole):
        k = self.groups
        self.groups += 1
        self.open.append((whole, k))
        return k

    def copy(self, k, src, dst, device):
        return pltpu.make_async_remote_copy(
            src_ref=src, dst_ref=dst, send_sem=self.send.at[k], recv_sem=self.recv.at[k],
            device_id=(device,), device_id_type=MESH,
        )

    def start(self, k, src, dst, device):
        self.copy(k, src, dst, device).start()

    def arrived(self, k):
        whole, _ = self.open[k]
        self.copy(k, whole, whole, lax.axis_index("dp")).wait_recv()

    def finish(self):
        for whole, k in self.open:
            self.copy(k, whole, whole, lax.axis_index("dp")).wait_send()


class Gather:
    def __init__(self, ref, copies, place):
        self.ref, self.copies, self.p = ref, copies, place

    def begin(self, own):
        ref, p = self.ref, self.p
        self.first = self.copies.group(ref.at[pl.ds(0, p.planes - 1), p.q, p.c])
        self.second = self.copies.group(ref.at[:, pl.ds(0, QUAD - 1), p.c])
        for a in range(1, p.planes):
            self.copies.start(self.first, own, ref.at[p.z, p.q, p.c], p.device(p.plane(a), p.q))
        for b in range(1, QUAD):
            self.copies.start(self.second, own, ref.at[p.z, p.q, p.c], p.device(p.z, p.corner(b)))

    def spread(self):
        ref, p = self.ref, self.p
        self.copies.arrived(self.first)
        for a in range(1, p.planes):
            part = ref.at[p.plane(a), p.q, p.c]
            for b in range(1, QUAD):
                self.copies.start(self.second, part, part, p.device(p.z, p.corner(b)))

    def pair(self):
        part = self.ref.at[:, :, self.p.c]
        self.copies.arrived(self.second)
        self.third = self.copies.group(part)
        self.copies.start(self.third, part, part, self.p.partner)

    def end(self):
        self.copies.arrived(self.third)


class GatherRows:
    def __init__(self, ref, copies, place):
        self.ref, self.copies, self.p = ref, copies, place

    def begin(self):
        ref, p = self.ref, self.p
        self.now = self.copies.group(ref.at[p.c, p.q, pl.ds(0, p.planes - 1)])
        own = ref.at[p.c, p.q, pl.ds(p.z, 1)]
        for a in range(1, p.planes):
            self.copies.start(self.now, own, own, p.device(p.plane(a), p.q))

    def spread(self):
        ref, p = self.ref, self.p
        self.end()
        self.now = self.copies.group(ref.at[p.c, pl.ds(0, QUAD - 1)])
        for b in range(1, QUAD):
            self.copies.start(self.now, ref.at[p.c, p.q], ref.at[p.c, p.q], p.device(p.z, p.corner(b)))

    def pair(self):
        part = self.ref.at[self.p.c]
        self.end()
        self.now = self.copies.group(part)
        self.copies.start(self.now, part, part, self.p.partner)

    def end(self):
        self.copies.arrived(self.now)


def cut(values):
    half = values.shape[-1] // 2
    return jnp.concatenate([values[..., :half], values[..., half:]], axis=-2)


def uncut(values):
    return jnp.concatenate([values[..., :8, :], values[..., 8:, :]], axis=-1)


def same(values):
    return values


class Share:
    def __init__(self, r, name, cutter, copies, place, plane_first):
        self.r, self.name, self.cut, self.copies, self.p = r, name, cutter, copies, place
        self.plane_first = plane_first

    def ref(self, kind):
        return getattr(self.r, kind + self.name)

    def mine(self, ref):
        return ref[self.p.z] if self.plane_first else ref[:, self.p.q]

    def send(self, ref, target, along_planes):
        p = self.p
        self.now = self.copies.group(target)
        for k in range(1, p.planes if along_planes else QUAD):
            if along_planes:
                part, device = p.plane(k), p.device(p.plane(k), p.q)
            else:
                part, device = p.corner(k), p.device(p.z, p.corner(k))
            source = ref.at[:, part] if len(ref.shape) == 4 and not along_planes else ref.at[part]
            self.copies.start(self.now, source, target.at[k - 1], device)

    def pair(self):
        p = self.p
        self.ref("cs")[...] = self.cut(self.ref("dw")[:, :, 1 - p.c]).astype(BF16)
        self.now = self.copies.group(self.ref("cr"))
        self.copies.start(self.now, self.ref("cs"), self.ref("cr"), p.partner)

    def spread(self):
        self.copies.arrived(self.now)
        total = self.cut(self.ref("dw")[:, :, self.p.c]) + self.ref("cr")[...].astype(F32)
        self.ref("xs")[...] = total.astype(BF16)
        self.send(self.ref("xs"), self.ref("xr"), self.plane_first)

    def climb(self):
        p = self.p
        self.copies.arrived(self.now)
        own = self.ref("dw")[p.z, :, p.c] if self.plane_first else self.ref("dw")[:, p.q, p.c]
        total = self.cut(own) + self.mine(self.ref("cr")).astype(F32)
        for k in range(self.ref("xr").shape[0]):
            total = total + self.ref("xr")[k].astype(F32)
        self.ref("ac")[...] = total
        self.ref("zs")[...] = total.astype(BF16)
        self.send(self.ref("zs"), self.ref("zr"), not self.plane_first)

    def land(self):
        self.copies.arrived(self.now)
        total = self.ref("ac")[self.p.q if self.plane_first else self.p.z]
        for k in range(self.ref("zr").shape[0]):
            total = total + self.ref("zr")[k].astype(F32)
        return total


def share_space(name, n, rows, columns, cutting, plane_first):
    Z, v = n // (2 * QUAD), pltpu.VMEM
    R, C = (2 * rows, columns // 2) if cutting else (rows, columns)
    first, second = (Z, QUAD) if plane_first else (QUAD, Z)
    return {
        "dw" + name: v((Z, QUAD, 2, rows, columns), F32),
        "cs" + name: v((Z, QUAD, R, C), BF16),
        "cr" + name: v((Z, QUAD, R, C), BF16),
        "xs" + name: v((Z, QUAD, R, C), BF16),
        "xr" + name: v((first - 1, second, R, C), BF16),
        "ac" + name: v((second, R, C), F32),
        "zs" + name: v((second, R, C), BF16),
        "zr" + name: v((second - 1, R, C), BF16),
    }


def segments(n, D, FF):
    found, lane, offset = [], 0, 0
    for name, width in zip(("bb", "bh", "g1", "b1", "g2", "b2", "bu", "bd"), sum_widths(D, FF)):
        found.append((name, lane, width, width // n, offset))
        lane, offset = lane + width, offset + width // n
    return found


def fill_pick(r, n, D, FF):
    for name, lane, width, own, offset in segments(n, D, FF):
        l = lax.broadcasted_iota(jnp.int32, (width, 128), 0).astype(F32)
        k = lax.broadcasted_iota(jnp.int32, (width, 128), 1).astype(F32)
        place = l - own * jnp.floor((l + 0.5) * (1.0 / own)) + offset
        r.pick[pl.ds(lane, width), :] = jnp.where(place == k, 1.0, 0.0).astype(BF16)


def owners(n, D, FF):
    parts, Z = [], n // (2 * QUAD)
    for name, lane, width, own, offset in segments(n, D, FF):
        l = lax.broadcasted_iota(jnp.int32, (n, width), 1).astype(F32)
        row = lax.broadcasted_iota(jnp.int32, (n, width), 0)
        z, q, c = row % Z, row // Z % QUAD, row // (Z * QUAD)
        device = ((z * QUAD + q) * 2 + c).astype(F32)
        parts.append(jnp.floor((l + 0.5) * (1.0 / own)) == device)
    return jnp.concatenate(parts, axis=1)


ROWS = ("gback", "gheads", "gup", "gdown", "gvec")
OWN = tuple("own_" + name for name in ("bb", "bh", "g1", "b1", "g2", "b2", "bu", "bd"))
INPUTS = ("lengths", "x_hbm", "cot_hbm", "wb_own", "wh_own", "wu_own", "wd_own") + OWN
OUTPUTS = ("out", "ig") + ROWS


def mega(names, dims, n, FF, *refs):
    r = refs_of(names, refs)
    r.x, r.cot = r.out, r.ig
    S, L, D = dims
    nb = L // BLK
    p = Place(n)
    copies = Copies(r.send, r.recv)

    def run(f, first, last, down=False):
        def step(i, c):
            f(nb - 1 - i if down else i, r, dims)
            return c
        lax.fori_loop(first, last, step, 0, unroll=True)

    barrier = pltpu.get_barrier_semaphore()
    for peer in p.peers():
        pl.semaphore_signal(barrier, inc=1, device_id=(peer,), device_id_type=MESH)

    loads = [
        pltpu.make_async_copy(src, dst, r.local.at[k])
        for k, (src, dst) in enumerate((
            (r.wh_own, r.wh_mine), (r.wu_own, r.wu_mine),
            *((getattr(r, name), getattr(r, "my_" + name)) for name in OWN),
            (r.wb_own, r.wb.at[p.z, p.q, p.c]), (r.wd_own, r.wd.at[p.z, p.q, p.c]),
            (r.x_hbm, r.x), (r.cot_hbm, r.cot),
        ))
    ]
    for load in loads:
        load.start()
    wb, wh, wu, wd = (Gather(ref, copies, p) for ref in (r.wb, r.wh_cut, r.wu_cut, r.wd))
    vec = GatherRows(r.vec, copies, p)
    pl.semaphore_wait(barrier, len(p.peers()))
    wb.begin(r.wb_own)
    r.vec_rows[...] = jnp.zeros_like(r.vec_rows)
    for load in loads[:-4]:
        load.wait()
    own_row = jnp.zeros((1, 128), F32)
    for k, (name, lane, width, own, offset) in enumerate(segments(n, D, FF)):
        r.vec_rows[pl.ds(k, 1), pl.ds(0, own)] = getattr(r, "my_" + OWN[k])[...].astype(F32)
        own_row = own_row + pltpu.roll(r.vec_rows[pl.ds(k, 1), :], offset, 1)
    r.vec[p.c, p.q, pl.ds(p.z, 1)] = own_row
    r.wh_cut[p.z, p.q, p.c] = cut(r.wh_mine[...].astype(F32)).astype(BF16)
    r.wu_cut[p.z, p.q, p.c] = cut(r.wu_mine[...].astype(F32)).astype(BF16)
    vec.begin()
    wh.begin(r.wh_cut.at[p.z, p.q, p.c])
    set_up(r)
    wb.spread()
    vec.spread()
    wh.spread()
    wu.begin(r.wu_cut.at[p.z, p.q, p.c])
    wd.begin(r.wd_own)
    for load in loads[-4:]:
        load.wait()
    run(enter, 0, nb)
    fill_pick(r, n, D, FF)
    wb.pair()
    vec.pair()
    wu.spread()
    wd.spread()
    wb.end()
    vec.end()
    spread = mm_nt(r.vec[...].reshape(n, 128).astype(BF16), r.pick[...])
    vectors = jnp.sum(jnp.where(owners(n, D, FF), spread, 0.0), axis=0, keepdims=True)
    for name, lane, width, own, offset in segments(n, D, FF):
        getattr(r, name)[...] = vectors[:, lane : lane + width]

    run(backbone, 0, nb)
    wh.pair()
    wh.end()
    r.wh[...] = uncut(r.wh_cut[...].astype(F32)).reshape(D, 3 * D).astype(BF16)
    run(gates, 0, nb)
    wu.pair()
    run(norms, 0, nb)
    wu.end()
    r.wu[...] = uncut(r.wu_cut[...].astype(F32)).reshape(D, FF).astype(BF16)
    wd.pair()
    up = Share(r, "u", cut, copies, p, UP_PLANE)
    down = Share(r, "d", same, copies, p, DOWN_PLANE)
    heads = Share(r, "h", cut, copies, p, HEADS_PLANE)
    back = Share(r, "b", same, copies, p, BACK_PLANE)

    def turn_down():
        r.dwd[...] = r.dwd_t[...].T.reshape(r.dwd.shape)

    middle(r, dims, {
        0: (wd.end,),
        nb - 1: (turn_down, down.pair),
        nb: (up.pair, down.spread),
        nb + 1: (up.spread,),
    })
    heads.pair()
    back.pair()

    rest, rows = jnp.where(owners(n, D, FF), column_sums(r), 0.0), None
    for _ in range(3):
        part = rest.astype(BF16)
        rest = rest - part.astype(F32)
        row = mm(part, r.pick[...])
        rows = row if rows is None else rows + row
    r.vs[...] = rows.reshape(r.vs.shape)
    vec_out = copies.group(r.vr)
    copies.start(vec_out, r.vs.at[1 - p.c], r.vr, p.partner)
    heads.spread()
    back.spread()
    copies.arrived(vec_out)
    r.va[...] = r.vs[p.c] + r.vr[...]
    vec_out = copies.group(r.vx)
    for b in range(1, QUAD):
        q = p.corner(b)
        copies.start(vec_out, r.va.at[q], r.vx.at[b - 1], p.device(p.z, q))
    down.climb()
    up.climb()
    run(leave, 0, nb, True)
    heads.climb()
    back.climb()
    copies.arrived(vec_out)
    total = r.va[p.q]
    for b in range(QUAD - 1):
        total = total + r.vx[b]
    r.vz[...] = total
    vec_out = copies.group(r.vt)
    for a in range(1, p.planes):
        z = p.plane(a)
        copies.start(vec_out, r.vz.at[pl.ds(z, 1)], r.vt.at[pl.ds(a - 1, 1)], p.device(z, p.q))
    run(emit, 0, nb)
    r.gup[...] = uncut(up.land())
    r.gdown[...] = down.land()
    r.gheads[...] = uncut(heads.land())
    r.gback[...] = back.land()
    copies.arrived(vec_out)
    r.gvec[...] = r.vz[pl.ds(p.z, 1), :] + jnp.sum(r.vt[...], axis=0, keepdims=True)
    copies.finish()


def quick(lengths, x, cot, wb, wh, wu, wd, vectors, n):
    vectors = [v.reshape(1, -1) for v in vectors]
    S = lengths.shape[0]
    T, D = x.shape
    L, FF = T // S, wu.shape[1]
    Z, v = n // (2 * QUAD), pltpu.VMEM
    space = work_space(S, L, D, FF)
    rb, rh, ru, rd = wb.shape[0], wh.shape[0], wu.shape[0], wd.shape[0]
    space.update(
        wb=v((Z, QUAD, 2, rb, D), BF16), wd=v((Z, QUAD, 2, rd, D), BF16),
        wh_cut=v((Z, QUAD, 2, 2 * rh, 3 * D // 2), BF16), wu_cut=v((Z, QUAD, 2, 2 * ru, FF // 2), BF16),
        wh=v((D, 3 * D), BF16), wu=v((D, FF), BF16), wh_mine=v((rh, 3 * D), BF16), wu_mine=v((ru, FF), BF16),
        vec=v((2, QUAD, Z, 128), F32), pick=v((sum(sum_widths(D, FF)), 128), BF16),
        vs=v((2, QUAD, Z, 128), F32), vr=v((QUAD, Z, 128), F32), va=v((QUAD, Z, 128), F32),
        vx=v((QUAD - 1, Z, 128), F32), vz=v((Z, 128), F32), vt=v((Z - 1, 128), F32),
        local=pltpu.SemaphoreType.DMA((14,)), send=pltpu.SemaphoreType.DMA((30,)), recv=pltpu.SemaphoreType.DMA((30,)),
    )
    for name, lane, width, own, offset in segments(n, D, FF):
        space[name] = v((1, width), F32)
        space["my_own_" + name] = v((1, own), BF16)
    space["vec_rows"] = v((8, 128), F32)
    space.update(share_space("u", n, ru, FF, True, UP_PLANE))
    space.update(share_space("d", n, rd, D, False, DOWN_PLANE))
    space.update(share_space("h", n, rh, 3 * D, True, HEADS_PLANE))
    space.update(share_space("b", n, rb, D, False, BACK_PLANE))
    shapes = (
        v((T, D), BF16), v((T, D), BF16),
        v((rb, D), F32), v((rh, 3 * D), F32), v((ru, FF), F32), v((rd, D), F32), v((1, 128), F32),
    )
    hbm, vmem = pl.BlockSpec(memory_space=pl.ANY), pl.BlockSpec(memory_space=pltpu.VMEM)
    results = pl.pallas_call(
        functools.partial(mega, INPUTS + OUTPUTS + tuple(space), (S, L, D), n, FF),
        out_shape=shapes,
        in_specs=[pl.BlockSpec(memory_space=pltpu.SMEM)] + [hbm] * 14,
        out_specs=[vmem] * 7,
        scratch_shapes=list(space.values()),
        compiler_params=pltpu.CompilerParams(collective_id=0, has_side_effects=True, vmem_limit_bytes=60 << 20),
    )(lengths, x, cot, wb, wh, wu, wd, *vectors)
    return hand_over(results, [own for name, lane, width, own, offset in segments(n, D, FF)])


def hand_over_kernel(widths, *refs):
    count = 6
    sources, vec, targets = refs[:count], refs[count], refs[count + 1 : 2 * count + 1]
    smalls, sem = refs[2 * count + 1 : -1], refs[-1]
    moves = [pltpu.make_async_copy(s, t, sem.at[k]) for k, (s, t) in enumerate(zip(sources, targets))]
    for move in moves:
        move.start()
    at = 0
    for small, width in zip(smalls, widths):
        small[...] = pltpu.roll(vec[...], (128 - at) % 128, 1)[:, :width]
        at += width
    for move in moves:
        move.wait()


def hand_over(results, widths):
    hbm, vmem = pl.BlockSpec(memory_space=pl.ANY), pl.BlockSpec(memory_space=pltpu.VMEM)
    shapes = [jax.ShapeDtypeStruct(a.shape, a.dtype) for a in results[:6]]
    shapes += [jax.ShapeDtypeStruct((1, w), F32) for w in widths]
    return pl.pallas_call(
        functools.partial(hand_over_kernel, widths),
        out_shape=shapes,
        in_specs=[vmem] * 7,
        out_specs=[hbm] * 6 + [vmem] * len(widths),
        scratch_shapes=[pltpu.SemaphoreType.DMA((6,))],
        compiler_params=pltpu.CompilerParams(vmem_limit_bytes=16 << 20),
    )(*results)


def plain(names, dims, *refs):
    r = refs_of(names, refs)
    S, L, D = dims
    nb = L // BLK

    def run(f, down=False):
        def step(i, c):
            f(nb - 1 - i if down else i, r, dims)
            return c
        lax.fori_loop(0, nb, step, 0)

    set_up(r)
    for f in (enter, backbone, gates, norms):
        run(f)
    middle(r, dims, {})
    run(emit)
    run(leave, True)
    r.gdown[...] = r.dwd_t[...].T
    sums, at = column_sums(r), 0
    for name in SUMS:
        ref = getattr(r, "all" + name)
        ref[...] = sums[:, at : at + ref.shape[1]]
        at += ref.shape[1]


def whole(lengths, x, cot, matrices, vectors):
    S = lengths.shape[0]
    T, D = x.shape
    L, FF = T // S, matrices[2].shape[1]
    space = work_space(S, L, D, FF)
    names = ("lengths", "x", "cot", "wb", "wh", "wu", "wd", "bb", "bh", "g1", "b1", "g2", "b2", "bu", "bd")
    names += ("out", "ig", "dwb", "dwh", "dwu", "gdown") + tuple("all" + name for name in SUMS) + tuple(space)
    row = lambda a, b: jax.ShapeDtypeStruct((a, b), F32)
    shapes = (jax.ShapeDtypeStruct((T, D), BF16),) * 2
    shapes += tuple(row(*m.shape) for m in matrices) + tuple(row(1, width) for width in sum_widths(D, FF))
    vmem = pl.BlockSpec(memory_space=pltpu.VMEM)
    return pl.pallas_call(
        functools.partial(plain, names, (S, L, D)),
        out_shape=shapes,
        in_specs=[pl.BlockSpec(memory_space=pltpu.SMEM)] + [vmem] * 14,
        out_specs=[vmem] * len(shapes),
        scratch_shapes=list(space.values()),
        compiler_params=pltpu.CompilerParams(vmem_limit_bytes=62 << 20),
    )(lengths, x, cot, *matrices, *(v.astype(F32).reshape(1, -1) for v in vectors))


def by_collectives(lengths, x, cot, matrices, vectors):
    gather = lambda a: lax.all_gather(a, "dp", axis=0, tiled=True)
    scatter = lambda a: lax.psum_scatter(a, "dp", scatter_dimension=0, tiled=True)
    results = whole(lengths, x, cot, [gather(m) for m in matrices], [gather(v) for v in vectors])
    return results[:2], [scatter(m) for m in results[2:6]], [scatter(v[0]) for v in results[6:]]


def by_kernel(lengths, x, cot, matrices, vectors, n):
    results = quick(lengths, x, cot, *matrices, vectors, n)
    return results[:2], results[2:6], [row[0] for row in results[6:]]


def in_tiles(n, back_w, heads_w, up_w, down_w):
    rows = 2 * QUAD * down_w.shape[0]
    return (
        n % (2 * QUAD) == 0 and heads_w.shape[0] == 8 and up_w.shape[0] == 8
        and back_w.shape[0] % 16 == 0 and down_w.shape[0] % 16 == 0 and FF_STEP % rows == 0
    )


def local(n, block_in, lengths, back_w, back_b, heads_w, heads_b, norm1_gain, norm1_bias, norm2_gain, norm2_bias,
          up_w, up_b, down_w, down_b, cotangent):
    matrices = (back_w, heads_w, up_w, down_w)
    vectors = (back_b, heads_b, norm1_gain, norm1_bias, norm2_gain, norm2_bias, up_b, down_b)
    if in_tiles(n, *matrices):
        big, weights, small = by_kernel(lengths, block_in, cotangent, matrices, vectors, n)
    else:
        big, weights, small = by_collectives(lengths, block_in, cotangent, matrices, vectors)
    gback, gheads, gup, gdown = weights
    gb, gh, gg1, gb1, gg2, gb2, gu, gd = small
    return *big, gback, gb, gheads, gh, gg1, gb1, gg2, gb2, gup, gu, gdown, gd


def solution(mesh):
    n = mesh.shape["dp"]
    m, v = P("dp", None), P("dp")
    return jax.shard_map(
        functools.partial(local, n), mesh=mesh,
        in_specs=(m, v, m, v, m, v, v, v, v, v, m, v, m, v, m),
        out_specs=(m, m, m, v, m, v, v, v, v, v, m, v, m, v), check_vma=False,
    )
```

```python
import functools

import jax
import jax.numpy as jnp
from jax import lax
from jax.experimental import pallas as pl
from jax.experimental.pallas import tpu as pltpu
from jax.sharding import PartitionSpec as P

BLK = 256
LANES = 8
STEPS = BLK // LANES
QUAD = 4
FF_STEP = 256
UP_PLANE, DOWN_PLANE, HEADS_PLANE, BACK_PLANE = False, False, False, True
F32 = jnp.float32
BF16 = jnp.bfloat16
MESH = pl.DeviceIdType.MESH
GC = 0.7978845608028654
GA = 0.044715


def mm(a, b):
    return lax.dot_general(a, b, (((1,), (0,)), ((), ())), preferred_element_type=F32)


def mm_nt(a, b):
    return lax.dot_general(a, b, (((1,), (1,)), ((), ())), preferred_element_type=F32)


def shuffle(transposed=False):
    row = lax.broadcasted_iota(jnp.int32, (BLK, BLK), 0)
    col = lax.broadcasted_iota(jnp.int32, (BLK, BLK), 1)
    if transposed:
        row, col = col, row
    return jnp.where((row & 7) * STEPS + (row >> 3) == col, 1.0, 0.0).astype(BF16)


def fold(values):
    return jnp.sum(values.reshape(values.shape[0] // 8, 8, values.shape[1]), axis=0)


def sublane(shape):
    return lax.broadcasted_iota(jnp.int32, shape, 0)


def flat(ref):
    values = ref[...]
    return values.reshape(-1, values.shape[-1])


def block_rows(i, dims):
    return pl.ds(pl.multiple_of(i * (dims[0] * BLK), dims[0] * BLK), dims[0] * BLK)


def add_to(ref, columns, values):
    ref[..., columns] += values.reshape(ref.shape[:-1] + values.shape[-1:])


def live(i, r, dims):
    S, L, D = dims
    row = lax.broadcasted_iota(jnp.int32, (BLK, D), 0)
    time = (row & 7) * STEPS + (row >> 3) + i * BLK
    return jnp.concatenate([time < r.lengths[s] for s in range(S)], axis=0)


def enter(i, r, dims):
    S, L, D = dims
    order = shuffle()
    sub = sublane((8, D))
    joined, cots = [], []
    for s in range(S):
        cots.append(mm(order, r.cot[pl.ds(s * L + i * BLK, BLK), :]))
        mixed = mm(order, r.x[pl.ds(s * L + i * BLK, BLK), :])
        turned = pltpu.roll(mixed[BLK - 8 :], 1, 0)
        first = jnp.where(sub == 0, jnp.where(i == 0, 0.0, r.xcarry[s]), turned)
        r.xcarry[s] = turned
        before = jnp.concatenate([first, mixed[: BLK - 8]], axis=0)
        joined.append(jnp.concatenate([mixed, before], axis=1))
    rows = block_rows(i, dims)
    joined = jnp.concatenate(joined, axis=0).astype(BF16)
    r.joined[rows, :] = joined
    r.joined_t[pl.ds(0, 2 * D), rows] = joined.T
    cot = jnp.concatenate(cots, axis=0)
    r.mixed_cot[rows, :] = cot.astype(BF16)
    gout = jnp.where(live(i, r, dims), cot, 0.0)
    r.gbd[...] += fold(gout)
    half = (0.5 * gout).astype(BF16)
    r.half[rows, :] = half
    r.half_t[:, rows] = half.T


def backbone(i, r, dims):
    S, L, D = dims
    rows = block_rows(i, dims)
    inner = jnp.tanh(0.666 * (mm(r.joined[rows, :], flat(r.wb)) + r.bb[...]))
    r.bend[rows, :] = (1.7159 * 0.666) * (1.0 - inner * inner)
    feat = (1.7159 * inner).astype(BF16)
    r.feat[rows, :] = feat
    r.feat_t[pl.ds(0, D), rows] = feat.T


def gates(i, r, dims):
    S, L, D = dims
    rows = block_rows(i, dims)
    sub = sublane((8, D))
    heads = mm(r.feat[rows, :], r.wh[...]) + r.bh[...]
    o = 0.5 * jnp.tanh(0.5 * heads[:, :D]) + 0.5
    v = jnp.tanh(heads[:, D : 2 * D])
    f = jnp.tanh(heads[:, 2 * D :])
    keep = 1.0 - o
    drive = f + o * (v - f)
    r.keep[rows, :] = keep
    r.v[rows, :] = v
    r.f[rows, :] = f
    one = jnp.ones((8, D), F32)
    for s in range(S):
        k = [keep[s * BLK + 8 * j : s * BLK + 8 * j + 8] for j in range(STEPS)]
        d = [drive[s * BLK + 8 * j : s * BLK + 8 * j + 8] for j in range(STEPS)]
        A, Q = k[0], d[0]
        for j in range(1, STEPS):
            Q = k[j] * Q + d[j]
            A = k[j] * A
        for sh in (1, 2, 4):
            An = jnp.where(sub < sh, one, pltpu.roll(A, sh, 0))
            Qn = jnp.where(sub < sh, 0.0, pltpu.roll(Q, sh, 0))
            Q = Q + A * Qn
            A = A * An
        carry = jnp.where(i == 0, 0.0, r.scarry[s])
        ends = Q + A * carry
        r.scarry[s] = jnp.broadcast_to(ends[7:8], (8, D))
        Q = jnp.where(sub == 0, carry, pltpu.roll(ends, 1, 0))
        r.start[i, s] = Q
        for j in range(STEPS):
            at = s * BLK + 8 * j
            place = pl.ds(pl.multiple_of(i * (S * BLK) + at, 8), 8)
            Q = k[j] * Q + d[j]
            r.state[place, :] = Q


def normalise(values, D):
    c = values - jnp.sum(values, axis=1, keepdims=True) * (1.0 / D)
    rs = lax.rsqrt(jnp.sum(c * c, axis=1, keepdims=True) + 1e-05 * D)
    return c * rs, rs


def norms(i, r, dims):
    S, L, D = dims
    rows = block_rows(i, dims)
    xhat1, rs1 = normalise(r.state[rows, :], D)
    branch = jnp.where(live(i, r, dims), xhat1 * r.g1[...] + r.b1[...], 0.0)
    mid = r.joined[rows, pl.ds(0, D)].astype(F32) + branch
    xhat2, rs2 = normalise(mid, D)
    normed = (xhat2 * r.g2[...] + r.b2[...]).astype(BF16)
    r.xhat1[rows, :] = xhat1
    r.xhat2[rows, :] = xhat2
    r.rs1[rows, :] = rs1
    r.rs2[rows, :] = rs2
    r.mid[rows, :] = mid
    r.normed[rows, :] = normed
    r.normed_t[pl.ds(0, D), rows] = normed.T


def feed_up(i, n, r, dims):
    rows, cols = block_rows(i, dims), slice(n * FF_STEP, (n + 1) * FF_STEP)
    pu = mm(r.normed[rows, :], r.wu[:, cols]) + r.bu[:, cols]
    v2 = pu * pu
    s = 1.0 + jnp.tanh(pu * (v2 * (GC * GA) + GC))
    hid = pu * s
    hid16 = hid.astype(BF16)
    r.hidden[rows, cols] = hid16
    r.slope[i % 2, :, cols] = s + hid * (2.0 - s) * (v2 * (3.0 * GA * GC) + GC)
    r.dwd_t[:, cols] += mm(r.half_t[:, rows], hid16)


def feed_down(i, n, r, dims):
    D = dims[2]
    rows, cols = block_rows(i, dims), slice(n * FF_STEP, (n + 1) * FF_STEP)
    gpu = (mm_nt(r.half[rows, :], r.wd_rows(n, FF_STEP)) * r.slope[i % 2, :, cols]).astype(BF16)
    r.gpu[i % 2, :, cols] = gpu
    part = mm(r.normed_t[:, rows], gpu)
    add_to(r.dwu, cols, part[:D])
    r.gbu[:, cols] += part[D : D + 8]


def norm_back(dx, xhat, rs, total, by_gain, D):
    ex = dx * xhat
    total[...] += fold(dx)
    by_gain[...] += fold(ex)
    m1 = jnp.sum(dx, axis=1, keepdims=True) * (1.0 / D)
    m2 = jnp.sum(ex, axis=1, keepdims=True)
    return rs * (dx - m1 - xhat * m2)


def norms_back(i, r, dims):
    S, L, D = dims
    rows = block_rows(i, dims)
    gn = mm_nt(r.gpu[i % 2], r.wu[...])
    gmid = r.mixed_cot[rows, :].astype(F32) + norm_back(gn * r.g2[...], r.xhat2[rows, :], r.rs2[rows, :], r.gb2, r.gg2, D)
    r.gmid[rows, :] = gmid
    dx = jnp.where(live(i, r, dims), gmid * r.g1[...], 0.0)
    r.gnorm[rows, :] = norm_back(dx, r.xhat1[rows, :], r.rs1[rows, :], r.gb1, r.gg1, D)


def gates_back(i, r, dims):
    S, L, D = dims
    nb = L // BLK
    rows = block_rows(i, dims)
    sub = sublane((8, D))
    keep = r.keep[rows, :]
    gnorm = r.gnorm[rows, :]
    gs = []
    one = jnp.ones((8, D), F32)
    for s in range(S):
        k = [keep[s * BLK + 8 * j : s * BLK + 8 * j + 8] for j in range(STEPS)]
        g = [gnorm[s * BLK + 8 * j : s * BLK + 8 * j + 8] for j in range(STEPS)]
        A = k[STEPS - 1]
        H = k[STEPS - 1] * g[STEPS - 1]
        for j in range(STEPS - 2, -1, -1):
            H = k[j] * (g[j] + H)
            A = k[j] * A
        for sh in (1, 2, 4):
            An = jnp.where(sub >= 8 - sh, one, pltpu.roll(A, 8 - sh, 0))
            Hn = jnp.where(sub >= 8 - sh, 0.0, pltpu.roll(H, 8 - sh, 0))
            H = H + A * Hn
            A = A * An
        carry = jnp.where(i == nb - 1, 0.0, r.scarry[s])
        ends = H + A * carry
        r.scarry[s] = jnp.broadcast_to(ends[0:1], (8, D))
        H = jnp.where(sub == 7, carry, pltpu.roll(ends, 7, 0))
        out = [None] * STEPS
        for j in range(STEPS - 1, -1, -1):
            out[j] = g[j] + H
            H = k[j] * out[j]
        gs += out
    gs = jnp.concatenate(gs, axis=0)
    before = []
    for s in range(S):
        before += [r.start[i, s], r.state[pl.ds(pl.multiple_of(i * (S * BLK) + s * BLK, BLK), BLK - 8), :]]
    before = jnp.concatenate(before, axis=0)
    v, f = r.v[rows, :], r.f[rows, :]
    go = gs * (1.0 - keep)
    grate = go * keep * (v - f - before)
    gph = jnp.concatenate([grate, go * (1.0 - v * v), (gs - go) * (1.0 - f * f)], axis=1).astype(BF16)
    gpb = (mm_nt(gph, r.wh[...]) * r.bend[rows, :]).astype(BF16)
    r.gpb[rows, :] = gpb
    part = mm(r.feat_t[:, rows], gph)
    add_to(r.dwh, slice(0, 3 * D), part[:D])
    r.gbh[...] += part[D : D + 8]
    part = mm(r.joined_t[:, rows], gpb)
    add_to(r.dwb, slice(0, D), part[: 2 * D])
    r.gbb[...] += part[2 * D : 2 * D + 8]


def middle(r, dims, after):
    nb = dims[1] // BLK
    for step in range(nb + 1):
        for n in range(r.wu.shape[1] // FF_STEP):
            if step < nb:
                feed_up(nb - 1 - step, n, r, dims)
            if 0 <= step - 1 < nb:
                feed_down(nb - 1 - (step - 1), n, r, dims)
        if step:
            norms_back(nb - step, r, dims)
        for action in after.get(step, ()):
            action()
    for i in reversed(range(nb)):
        gates_back(i, r, dims)
        if i == nb // 2:
            for action in after.get(nb + 1, ()):
                action()


def emit(i, r, dims):
    S, L, D = dims
    rows = block_rows(i, dims)
    back = shuffle(True)
    branch = 0.5 * mm(r.hidden[rows, :], flat(r.wd)) + r.bd[...]
    out = (r.mid[rows, :] + jnp.where(live(i, r, dims), branch, 0.0)).astype(BF16)
    for s in range(S):
        r.out[pl.ds(s * L + i * BLK, BLK), :] = mm(back, out[s * BLK : (s + 1) * BLK]).astype(BF16)


def leave(i, r, dims):
    S, L, D = dims
    nb = L // BLK
    rows = block_rows(i, dims)
    sub = sublane((8, D))
    back = shuffle(True)
    gj = mm_nt(r.gpb[rows, :], flat(r.wb))
    gmid = r.gmid[rows, :]
    for s in range(S):
        own = gj[s * BLK : (s + 1) * BLK, :D]
        before = gj[s * BLK : (s + 1) * BLK, D:]
        turned = pltpu.roll(before[:8], 7, 0)
        last = jnp.where(sub == 7, jnp.where(i == nb - 1, 0.0, r.xcarry[s]), turned)
        r.xcarry[s] = turned
        moved = jnp.concatenate([before[8:], last], axis=0)
        grad = (gmid[s * BLK : (s + 1) * BLK] + own + moved).astype(BF16)
        r.ig[pl.ds(s * L + i * BLK, BLK), :] = mm(back, grad).astype(BF16)


SUMS = ("gbb", "gbh", "gg1", "gb1", "gg2", "gb2", "gbu", "gbd")


def set_up(r):
    for name in SUMS + ("dwu", "dwd_t", "dwh", "dwb"):
        ref = getattr(r, name)
        ref[...] = jnp.zeros_like(ref)
    for ref in (r.joined_t, r.feat_t, r.normed_t):
        ref[pl.ds(ref.shape[0] - 16, 16), :] = jnp.ones((16, ref.shape[1]), BF16)


def column_sums(r):
    parts = []
    for name in SUMS:
        if name in ("gbb", "gbh", "gbu"):
            parts.append(getattr(r, name)[0:1, :])
        else:
            part = jnp.sum(getattr(r, name)[...], axis=0, keepdims=True)
            gain = {"gg1": r.g1, "gb1": r.g1, "gg2": r.g2, "gb2": r.g2}.get(name)
            if name in ("gg1", "gg2"):
                part = part * part.shape[1] ** 0.5
            parts.append(part if gain is None else part / gain[...])
    return jnp.concatenate(parts, axis=1)


def sum_widths(D, FF):
    return (D, 3 * D, D, D, D, D, FF, D)


def work_space(S, L, D, FF):
    T = S * L
    v = pltpu.VMEM
    space = dict(
        joined=v((T, 2 * D), BF16), joined_t=v((2 * D + 16, T), BF16), mixed_cot=v((T, D), BF16),
        half=v((T, D), BF16), half_t=v((D, T), BF16), bend=v((T, D), F32),
        feat=v((T, D), BF16), feat_t=v((D + 16, T), BF16), keep=v((T, D), F32),
        v=v((T, D), F32), f=v((T, D), F32), state=v((T, D), F32), gnorm=v((T, D), F32), start=v((L // BLK, S, 8, D), F32),
        xcarry=v((S, 8, D), F32), scarry=v((S, 8, D), F32), xhat1=v((T, D), F32), xhat2=v((T, D), F32),
        rs1=v((T, 1), F32), rs2=v((T, 1), F32), mid=v((T, D), F32), normed=v((T, D), BF16),
        normed_t=v((D + 16, T), BF16), hidden=v((T, FF), BF16), slope=v((2, S * BLK, FF), F32),
        gpu=v((2, S * BLK, FF), BF16), dwd_t=v((D, FF), F32),
    )
    for name, width in zip(SUMS, sum_widths(D, FF)):
        space[name] = v((8, width), F32)
    return space


class Refs:
    def wd_rows(self, n, width):
        if len(self.wd.shape) == 2:
            return self.wd[pl.ds(n * width, width), :]
        z, q, c, piece, columns = self.wd.shape
        plane = q * c * piece
        return self.wd[pl.ds(n * width // plane, width // plane)].reshape(width, columns)


def refs_of(names, refs):
    r = Refs()
    for name, ref in zip(names, refs):
        setattr(r, name, ref)
    r.gmid, r.gpb = r.xhat2, r.feat
    return r


class Place:
    def __init__(self, n):
        self.n = n
        self.planes = n // (2 * QUAD)
        self.me = lax.axis_index("dp")
        self.c = self.me % 2
        self.q = (self.me // 2) % QUAD
        self.z = self.me // (2 * QUAD)
        self.partner = self.me + 1 - 2 * self.c

    def plane(self, k):
        return (self.z + k) % self.planes

    def corner(self, k):
        return (self.q + k) % QUAD

    def device(self, z, q):
        return (z * QUAD + q) * 2 + self.c

    def peers(self):
        found = [self.device(self.plane(a), self.q) for a in range(1, self.planes)]
        found += [self.device(self.z, self.corner(b)) for b in range(1, QUAD)]
        return found + [self.partner]


class Copies:
    def __init__(self, send, recv):
        self.send, self.recv, self.groups = send, recv, 0
        self.open = []

    def group(self, whole):
        k = self.groups
        self.groups += 1
        self.open.append((whole, k))
        return k

    def copy(self, k, src, dst, device):
        return pltpu.make_async_remote_copy(
            src_ref=src, dst_ref=dst, send_sem=self.send.at[k], recv_sem=self.recv.at[k],
            device_id=(device,), device_id_type=MESH,
        )

    def start(self, k, src, dst, device):
        self.copy(k, src, dst, device).start()

    def arrived(self, k):
        whole, _ = self.open[k]
        self.copy(k, whole, whole, lax.axis_index("dp")).wait_recv()

    def finish(self):
        for whole, k in self.open:
            self.copy(k, whole, whole, lax.axis_index("dp")).wait_send()


class Gather:
    def __init__(self, ref, copies, place, early):
        self.ref, self.copies, self.p, self.early = ref, copies, place, early

    def begin(self, own):
        ref, p = self.ref, self.p
        self.first = self.copies.group(ref.at[pl.ds(0, p.planes - 1), p.q, p.c])
        self.second = self.copies.group(ref.at[:, pl.ds(0, QUAD - 1), p.c])
        for a in range(1, p.planes):
            self.copies.start(self.first, own, ref.at[p.z, p.q, p.c], p.device(p.plane(a), p.q))
        for b in range(1, QUAD if self.early else 1):
            self.copies.start(self.second, own, ref.at[p.z, p.q, p.c], p.device(p.z, p.corner(b)))

    def spread(self):
        ref, p = self.ref, self.p
        self.copies.arrived(self.first)
        parts = [ref.at[p.plane(a), p.q, p.c] for a in range(1, p.planes)] if self.early else [ref.at[:, p.q, p.c]]
        for part in parts:
            for b in range(1, QUAD):
                self.copies.start(self.second, part, part, p.device(p.z, p.corner(b)))

    def pair(self):
        part = self.ref.at[:, :, self.p.c]
        self.copies.arrived(self.second)
        self.third = self.copies.group(part)
        self.copies.start(self.third, part, part, self.p.partner)

    def end(self):
        self.copies.arrived(self.third)


class GatherRows:
    def __init__(self, ref, copies, place):
        self.ref, self.copies, self.p = ref, copies, place

    def begin(self):
        ref, p = self.ref, self.p
        self.now = self.copies.group(ref.at[p.c, p.q, pl.ds(0, p.planes - 1)])
        own = ref.at[p.c, p.q, pl.ds(p.z, 1)]
        for a in range(1, p.planes):
            self.copies.start(self.now, own, own, p.device(p.plane(a), p.q))

    def spread(self):
        ref, p = self.ref, self.p
        self.end()
        self.now = self.copies.group(ref.at[p.c, pl.ds(0, QUAD - 1)])
        for b in range(1, QUAD):
            self.copies.start(self.now, ref.at[p.c, p.q], ref.at[p.c, p.q], p.device(p.z, p.corner(b)))

    def pair(self):
        part = self.ref.at[self.p.c]
        self.end()
        self.now = self.copies.group(part)
        self.copies.start(self.now, part, part, self.p.partner)

    def end(self):
        self.copies.arrived(self.now)


def cut(values):
    half = values.shape[-1] // 2
    return jnp.concatenate([values[..., :half], values[..., half:]], axis=-2)


def uncut(values):
    return jnp.concatenate([values[..., :8, :], values[..., 8:, :]], axis=-1)


def same(values):
    return values


class Share:
    def __init__(self, r, name, cutter, copies, place, plane_first):
        self.r, self.name, self.cut, self.copies, self.p = r, name, cutter, copies, place
        self.plane_first = plane_first

    def ref(self, kind):
        return getattr(self.r, kind + self.name)

    def mine(self, ref):
        return ref[self.p.z] if self.plane_first else ref[:, self.p.q]

    def send(self, ref, target, along_planes):
        p = self.p
        self.now = self.copies.group(target)
        for k in range(1, p.planes if along_planes else QUAD):
            if along_planes:
                part, device = p.plane(k), p.device(p.plane(k), p.q)
            else:
                part, device = p.corner(k), p.device(p.z, p.corner(k))
            source = ref.at[:, part] if len(ref.shape) == 4 and not along_planes else ref.at[part]
            self.copies.start(self.now, source, target.at[k - 1], device)

    def pair(self):
        p = self.p
        self.ref("cs")[...] = self.cut(self.ref("dw")[:, :, 1 - p.c]).astype(BF16)
        self.now = self.copies.group(self.ref("cr"))
        self.copies.start(self.now, self.ref("cs"), self.ref("cr"), p.partner)

    def spread(self):
        self.copies.arrived(self.now)
        total = self.cut(self.ref("dw")[:, :, self.p.c]) + self.ref("cr")[...].astype(F32)
        self.ref("xs")[...] = total.astype(BF16)
        self.send(self.ref("xs"), self.ref("xr"), self.plane_first)

    def climb(self):
        p = self.p
        self.copies.arrived(self.now)
        own = self.ref("dw")[p.z, :, p.c] if self.plane_first else self.ref("dw")[:, p.q, p.c]
        total = self.cut(own) + self.mine(self.ref("cr")).astype(F32)
        for k in range(self.ref("xr").shape[0]):
            total = total + self.ref("xr")[k].astype(F32)
        self.ref("ac")[...] = total
        self.ref("zs")[...] = total.astype(BF16)
        self.send(self.ref("zs"), self.ref("zr"), not self.plane_first)

    def land(self):
        self.copies.arrived(self.now)
        total = self.ref("ac")[self.p.q if self.plane_first else self.p.z]
        for k in range(self.ref("zr").shape[0]):
            total = total + self.ref("zr")[k].astype(F32)
        return total


def share_space(name, n, rows, columns, cutting, plane_first):
    Z, v = n // (2 * QUAD), pltpu.VMEM
    R, C = (2 * rows, columns // 2) if cutting else (rows, columns)
    first, second = (Z, QUAD) if plane_first else (QUAD, Z)
    return {
        "dw" + name: v((Z, QUAD, 2, rows, columns), F32),
        "cs" + name: v((Z, QUAD, R, C), BF16),
        "cr" + name: v((Z, QUAD, R, C), BF16),
        "xs" + name: v((Z, QUAD, R, C), BF16),
        "xr" + name: v((first - 1, second, R, C), BF16),
        "ac" + name: v((second, R, C), F32),
        "zs" + name: v((second, R, C), BF16),
        "zr" + name: v((second - 1, R, C), BF16),
    }


def segments(n, D, FF):
    found, lane, offset = [], 0, 0
    for name, width in zip(("bb", "bh", "g1", "b1", "g2", "b2", "bu", "bd"), sum_widths(D, FF)):
        found.append((name, lane, width, width // n, offset))
        lane, offset = lane + width, offset + width // n
    return found


def fill_pick(r, n, D, FF):
    for name, lane, width, own, offset in segments(n, D, FF):
        l = lax.broadcasted_iota(jnp.int32, (width, 128), 0).astype(F32)
        k = lax.broadcasted_iota(jnp.int32, (width, 128), 1).astype(F32)
        place = l - own * jnp.floor((l + 0.5) * (1.0 / own)) + offset
        r.pick[pl.ds(lane, width), :] = jnp.where(place == k, 1.0, 0.0).astype(BF16)


def fill_owned(r, n, D, FF):
    Z = n // (2 * QUAD)
    for name, lane, width, own, offset in segments(n, D, FF):
        l = lax.broadcasted_iota(jnp.int32, (n, width), 1).astype(F32)
        row = lax.broadcasted_iota(jnp.int32, (n, width), 0)
        z, q, c = row % Z, row // Z % QUAD, row // (Z * QUAD)
        device = ((z * QUAD + q) * 2 + c).astype(F32)
        r.owned[:, pl.ds(lane, width)] = jnp.where(jnp.floor((l + 0.5) * (1.0 / own)) == device, 1.0, 0.0)


ROWS = ("gback", "gheads", "gup", "gdown", "gvec")
OWN = tuple("own_" + name for name in ("bb", "bh", "g1", "b1", "g2", "b2", "bu", "bd"))
INPUTS = ("lengths", "x_hbm", "cot_hbm", "wb_own", "wh_own", "wu_own", "wd_own") + OWN
OUTPUTS = ("out", "ig") + ROWS


def mega(names, dims, n, FF, *refs):
    r = refs_of(names, refs)
    r.x, r.cot = r.out, r.ig
    S, L, D = dims
    nb = L // BLK
    p = Place(n)
    copies = Copies(r.send, r.recv)

    def run(f, first, last, down=False):
        def step(i, c):
            f(nb - 1 - i if down else i, r, dims)
            return c
        lax.fori_loop(first, last, step, 0, unroll=True)

    barrier = pltpu.get_barrier_semaphore()
    for peer in p.peers():
        pl.semaphore_signal(barrier, inc=1, device_id=(peer,), device_id_type=MESH)

    loads = [
        pltpu.make_async_copy(src, dst, r.local.at[k])
        for k, (src, dst) in enumerate((
            (r.wh_own, r.wh_mine), (r.wu_own, r.wu_mine),
            *((getattr(r, name), getattr(r, "my_" + name)) for name in OWN),
            (r.wb_own, r.wb.at[p.z, p.q, p.c]), (r.wd_own, r.wd.at[p.z, p.q, p.c]),
            (r.x_hbm, r.x), (r.cot_hbm, r.cot),
        ))
    ]
    for load in loads:
        load.start()
    wb, wh, wu, wd = (
        Gather(ref, copies, p, early)
        for ref, early in zip((r.wb, r.wh_cut, r.wu_cut, r.wd), (True, True, False, False))
    )
    vec = GatherRows(r.vec, copies, p)
    pl.semaphore_wait(barrier, len(p.peers()))
    wb.begin(r.wb_own)
    r.vec_rows[...] = jnp.zeros_like(r.vec_rows)
    for load in loads[:-4]:
        load.wait()
    own_row = jnp.zeros((1, 128), F32)
    for k, (name, lane, width, own, offset) in enumerate(segments(n, D, FF)):
        r.vec_rows[pl.ds(k, 1), pl.ds(0, own)] = getattr(r, "my_" + OWN[k])[...].astype(F32)
        own_row = own_row + pltpu.roll(r.vec_rows[pl.ds(k, 1), :], offset, 1)
    r.vec[p.c, p.q, pl.ds(p.z, 1)] = own_row
    r.wh_cut[p.z, p.q, p.c] = cut(r.wh_mine[...].astype(F32)).astype(BF16)
    r.wu_cut[p.z, p.q, p.c] = cut(r.wu_mine[...].astype(F32)).astype(BF16)
    vec.begin()
    wh.begin(r.wh_cut.at[p.z, p.q, p.c])
    set_up(r)
    for load in loads[-4:]:
        load.wait()
    run(enter, 0, nb)
    wb.spread()
    vec.spread()
    wh.spread()
    wu.begin(r.wu_cut.at[p.z, p.q, p.c])
    wd.begin(r.wd_own)
    fill_pick(r, n, D, FF)
    fill_owned(r, n, D, FF)
    wb.pair()
    vec.pair()
    wu.spread()
    wd.spread()
    wb.end()
    vec.end()
    spread = mm_nt(r.vec[...].reshape(n, 128).astype(BF16), r.pick[...])
    vectors = jnp.sum(r.owned[...] * spread, axis=0, keepdims=True)
    for name, lane, width, own, offset in segments(n, D, FF):
        held = vectors[:, lane : lane + width]
        getattr(r, name)[...] = held * D**0.5 if name in ("g1", "g2") else held

    run(backbone, 0, nb)
    wh.pair()
    wh.end()
    r.wh[...] = uncut(r.wh_cut[...].astype(F32)).reshape(D, 3 * D).astype(BF16)
    run(gates, 0, nb)
    wu.pair()
    run(norms, 0, nb)
    wu.end()
    r.wu[...] = uncut(r.wu_cut[...].astype(F32)).reshape(D, FF).astype(BF16)
    wd.pair()
    up = Share(r, "u", cut, copies, p, UP_PLANE)
    down = Share(r, "d", same, copies, p, DOWN_PLANE)
    heads = Share(r, "h", cut, copies, p, HEADS_PLANE)
    back = Share(r, "b", same, copies, p, BACK_PLANE)

    def turn_down():
        r.dwd[...] = r.dwd_t[...].T.reshape(r.dwd.shape)

    middle(r, dims, {
        0: (wd.end,),
        nb - 1: (turn_down, down.pair),
        nb: (up.pair, down.spread),
        nb + 1: (up.spread,),
    })
    heads.pair()
    back.pair()

    rest, rows = r.owned[...] * column_sums(r), None
    for _ in range(3):
        part = rest.astype(BF16)
        rest = rest - part.astype(F32)
        row = mm(part, r.pick[...])
        rows = row if rows is None else rows + row
    r.vs[...] = rows.reshape(r.vs.shape)
    vec_out = copies.group(r.vr)
    copies.start(vec_out, r.vs.at[1 - p.c], r.vr, p.partner)
    heads.spread()
    back.spread()
    copies.arrived(vec_out)
    r.va[...] = r.vs[p.c] + r.vr[...]
    vec_out = copies.group(r.vx)
    for b in range(1, QUAD):
        q = p.corner(b)
        copies.start(vec_out, r.va.at[q], r.vx.at[b - 1], p.device(p.z, q))
    down.climb()
    up.climb()
    run(leave, 0, nb, True)
    heads.climb()
    back.climb()
    copies.arrived(vec_out)
    total = r.va[p.q]
    for b in range(QUAD - 1):
        total = total + r.vx[b]
    r.vz[...] = total
    vec_out = copies.group(r.vt)
    for a in range(1, p.planes):
        z = p.plane(a)
        copies.start(vec_out, r.vz.at[pl.ds(z, 1)], r.vt.at[pl.ds(a - 1, 1)], p.device(z, p.q))
    run(emit, 0, nb)
    r.gup[...] = uncut(up.land())
    r.gdown[...] = down.land()
    r.gheads[...] = uncut(heads.land())
    r.gback[...] = back.land()
    copies.arrived(vec_out)
    r.gvec[...] = r.vz[pl.ds(p.z, 1), :] + jnp.sum(r.vt[...], axis=0, keepdims=True)
    copies.finish()


def quick(lengths, x, cot, wb, wh, wu, wd, vectors, n):
    vectors = [v.reshape(1, -1) for v in vectors]
    S = lengths.shape[0]
    T, D = x.shape
    L, FF = T // S, wu.shape[1]
    Z, v = n // (2 * QUAD), pltpu.VMEM
    space = work_space(S, L, D, FF)
    rb, rh, ru, rd = wb.shape[0], wh.shape[0], wu.shape[0], wd.shape[0]
    space.update(
        wb=v((Z, QUAD, 2, rb, D), BF16), wd=v((Z, QUAD, 2, rd, D), BF16),
        wh_cut=v((Z, QUAD, 2, 2 * rh, 3 * D // 2), BF16), wu_cut=v((Z, QUAD, 2, 2 * ru, FF // 2), BF16),
        wh=v((D, 3 * D), BF16), wu=v((D, FF), BF16), wh_mine=v((rh, 3 * D), BF16), wu_mine=v((ru, FF), BF16),
        vec=v((2, QUAD, Z, 128), F32), pick=v((sum(sum_widths(D, FF)), 128), BF16),
        owned=v((n, sum(sum_widths(D, FF))), F32),
        vs=v((2, QUAD, Z, 128), F32), vr=v((QUAD, Z, 128), F32), va=v((QUAD, Z, 128), F32),
        vx=v((QUAD - 1, Z, 128), F32), vz=v((Z, 128), F32), vt=v((Z - 1, 128), F32),
        local=pltpu.SemaphoreType.DMA((14,)), send=pltpu.SemaphoreType.DMA((30,)), recv=pltpu.SemaphoreType.DMA((30,)),
    )
    for name, lane, width, own, offset in segments(n, D, FF):
        space[name] = v((1, width), F32)
        space["my_own_" + name] = v((1, own), BF16)
    space["vec_rows"] = v((8, 128), F32)
    space.update(share_space("u", n, ru, FF, True, UP_PLANE))
    space.update(share_space("d", n, rd, D, False, DOWN_PLANE))
    space.update(share_space("h", n, rh, 3 * D, True, HEADS_PLANE))
    space.update(share_space("b", n, rb, D, False, BACK_PLANE))
    shapes = (
        v((T, D), BF16), v((T, D), BF16),
        v((rb, D), F32), v((rh, 3 * D), F32), v((ru, FF), F32), v((rd, D), F32), v((1, 128), F32),
    )
    hbm, vmem = pl.BlockSpec(memory_space=pl.ANY), pl.BlockSpec(memory_space=pltpu.VMEM)
    results = pl.pallas_call(
        functools.partial(mega, INPUTS + OUTPUTS + tuple(space), (S, L, D), n, FF),
        out_shape=shapes,
        in_specs=[pl.BlockSpec(memory_space=pltpu.SMEM)] + [hbm] * 14,
        out_specs=[vmem] * 7,
        scratch_shapes=list(space.values()),
        compiler_params=pltpu.CompilerParams(collective_id=0, has_side_effects=True, vmem_limit_bytes=60 << 20),
    )(lengths, x, cot, wb, wh, wu, wd, *vectors)
    return hand_over(results, [own for name, lane, width, own, offset in segments(n, D, FF)])


def hand_over_kernel(widths, *refs):
    count, small = 6, len(widths)
    sources, vec, targets = refs[:count], refs[count], refs[count + 1 : 2 * count + 1 + small]
    rows, sem = refs[2 * count + 1 + small : -1], refs[-1]
    at = 0
    for row, width in zip(rows, widths):
        row[...] = pltpu.roll(vec[...], (128 - at) % 128, 1)[:, :width]
        at += width
    moves = [pltpu.make_async_copy(s, t, sem.at[k]) for k, (s, t) in enumerate(zip(sources + rows, targets))]
    for move in moves:
        move.start()
    for move in moves:
        move.wait()


def hand_over(results, widths):
    hbm, vmem = pl.BlockSpec(memory_space=pl.ANY), pl.BlockSpec(memory_space=pltpu.VMEM)
    shapes = [jax.ShapeDtypeStruct(a.shape, a.dtype) for a in results[:6]]
    shapes += [jax.ShapeDtypeStruct((1, w), F32) for w in widths]
    return pl.pallas_call(
        functools.partial(hand_over_kernel, widths),
        out_shape=shapes,
        in_specs=[vmem] * 7,
        out_specs=[hbm] * len(shapes),
        scratch_shapes=[pltpu.VMEM((1, w), F32) for w in widths] + [pltpu.SemaphoreType.DMA((len(shapes),))],
        compiler_params=pltpu.CompilerParams(vmem_limit_bytes=16 << 20),
    )(*results)


def plain(names, dims, *refs):
    r = refs_of(names, refs)
    S, L, D = dims
    nb = L // BLK

    def run(f, down=False):
        def step(i, c):
            f(nb - 1 - i if down else i, r, dims)
            return c
        lax.fori_loop(0, nb, step, 0)

    set_up(r)
    for f in (enter, backbone, gates, norms):
        run(f)
    middle(r, dims, {})
    run(emit)
    run(leave, True)
    r.gdown[...] = r.dwd_t[...].T
    sums, at = column_sums(r), 0
    for name in SUMS:
        ref = getattr(r, "all" + name)
        ref[...] = sums[:, at : at + ref.shape[1]]
        at += ref.shape[1]


def whole(lengths, x, cot, matrices, vectors):
    S = lengths.shape[0]
    T, D = x.shape
    L, FF = T // S, matrices[2].shape[1]
    space = work_space(S, L, D, FF)
    rows = [v.astype(F32).reshape(1, -1) for v in vectors]
    rows[2], rows[4] = rows[2] * D**0.5, rows[4] * D**0.5
    names = ("lengths", "x", "cot", "wb", "wh", "wu", "wd", "bb", "bh", "g1", "b1", "g2", "b2", "bu", "bd")
    names += ("out", "ig", "dwb", "dwh", "dwu", "gdown") + tuple("all" + name for name in SUMS) + tuple(space)
    row = lambda a, b: jax.ShapeDtypeStruct((a, b), F32)
    shapes = (jax.ShapeDtypeStruct((T, D), BF16),) * 2
    shapes += tuple(row(*m.shape) for m in matrices) + tuple(row(1, width) for width in sum_widths(D, FF))
    vmem = pl.BlockSpec(memory_space=pltpu.VMEM)
    return pl.pallas_call(
        functools.partial(plain, names, (S, L, D)),
        out_shape=shapes,
        in_specs=[pl.BlockSpec(memory_space=pltpu.SMEM)] + [vmem] * 14,
        out_specs=[vmem] * len(shapes),
        scratch_shapes=list(space.values()),
        compiler_params=pltpu.CompilerParams(vmem_limit_bytes=62 << 20),
    )(lengths, x, cot, *matrices, *rows)


def by_collectives(lengths, x, cot, matrices, vectors):
    gather = lambda a: lax.all_gather(a, "dp", axis=0, tiled=True)
    scatter = lambda a: lax.psum_scatter(a, "dp", scatter_dimension=0, tiled=True)
    results = whole(lengths, x, cot, [gather(m) for m in matrices], [gather(v) for v in vectors])
    return results[:2], [scatter(m) for m in results[2:6]], [scatter(v[0]) for v in results[6:]]


def by_kernel(lengths, x, cot, matrices, vectors, n):
    results = quick(lengths, x, cot, *matrices, vectors, n)
    return results[:2], results[2:6], [row[0] for row in results[6:]]


def in_tiles(n, back_w, heads_w, up_w, down_w):
    rows = 2 * QUAD * down_w.shape[0]
    return (
        n % (2 * QUAD) == 0 and heads_w.shape[0] == 8 and up_w.shape[0] == 8
        and back_w.shape[0] % 16 == 0 and down_w.shape[0] % 16 == 0 and FF_STEP % rows == 0
    )


def local(n, block_in, lengths, back_w, back_b, heads_w, heads_b, norm1_gain, norm1_bias, norm2_gain, norm2_bias,
          up_w, up_b, down_w, down_b, cotangent):
    matrices = (back_w, heads_w, up_w, down_w)
    vectors = (back_b, heads_b, norm1_gain, norm1_bias, norm2_gain, norm2_bias, up_b, down_b)
    if in_tiles(n, *matrices):
        big, weights, small = by_kernel(lengths, block_in, cotangent, matrices, vectors, n)
    else:
        big, weights, small = by_collectives(lengths, block_in, cotangent, matrices, vectors)
    gback, gheads, gup, gdown = weights
    gb, gh, gg1, gb1, gg2, gb2, gu, gd = small
    return *big, gback, gb, gheads, gh, gg1, gb1, gg2, gb2, gup, gu, gdown, gd


def solution(mesh):
    n = mesh.shape["dp"]
    m, v = P("dp", None), P("dp")
    return jax.shard_map(
        functools.partial(local, n), mesh=mesh,
        in_specs=(m, v, m, v, m, v, v, v, v, v, m, v, m, v, m),
        out_specs=(m, m, m, v, m, v, v, v, v, v, m, v, m, v), check_vma=False,
    )
```
